256 devices in a mesh: sample: 2 (over core), depth: 128 (over x, y, z).
Axes of the slice: x: 4, y: 4, z: 8, core: 2. Of those that a mesh axis runs over, the one named last changes fastest.
Arguments:
- volumes: bfloat16 [2, 4, 256, 32, 256], P('sample', None, 'depth'), may hold values from -6 to 6
- conv_one: bfloat16 [3, 3, 3, 4, 16], replicated, may hold values from -0.625 to 0.625
- bias_one: float32 [16], replicated, may hold values from -3 to 3
- conv_two: bfloat16 [3, 3, 3, 16, 32], replicated, may hold values from -0.3125 to 0.3125
- bias_two: float32 [32], replicated, may hold values from -3 to 3
- cotangent: bfloat16 [2, 32, 128, 16, 128], P('sample', None, 'depth'), may hold values from -0.008239746 to 0.008239746
Outputs:
- activations: bfloat16 [2, 32, 128, 16, 128], P('sample', None, 'depth')
- grad_conv_one: float32 [3, 3, 3, 4, 16], replicated
- grad_bias_one: float32 [16], replicated
- grad_conv_two: float32 [3, 3, 3, 16, 32], replicated
- grad_bias_two: float32 [32], replicated
The draws below stay inside these ranges and needn't reach their ends.
All inputs are finite; a program needn't handle non-finite values.
Results may differ from the reference program's by a relative error of at most 0.0095.
Values may be sent and summed in bfloat16 or wider, within the bound.
No kernel may reach another device: no remote copies, remote signals or barrier semaphores. Data moves between devices by JAX's collectives and lax.ppermute only.
A program may use at most 128 MiB of HBM per device.

```python
import jax
import jax.numpy as jnp
from jax import lax

C_IN = 4
C_ONE = 16
C_TWO = 32
HEIGHT = 32
WIDTH = 256
VOLUMES = 2
DEPTH = 256


def steps_of(key, shape, split, least, largest):
    factor_of = 1.0
    for dim, parts in split:
        heights = jax.random.uniform(jax.random.fold_in(jax.random.fold_in(key, 6), dim), (parts,), jnp.float32, least / len(split), largest / len(split))
        factor_of = factor_of * jnp.repeat(jnp.exp(heights), shape[dim] // parts).reshape((-1,) + (1,) * (len(shape) - 1 - dim))
    return factor_of


def scatter_about(stream_key, extent, scale, bound, cuts=(), kind=jnp.bfloat16):
    result = jax.random.normal(stream_key, extent, jnp.float32) * scale
    if len(cuts) > 0:
        result = steps_of(stream_key, extent, cuts, -0.22, 0.18) * result
    return jnp.clip(result, min=-bound, max=bound).astype(kind)


def setup_inputs(seed: int = 0) -> dict:
    arg_keys = jax.random.split(jax.random.key(seed), 7)
    return {
        "volumes": scatter_about(arg_keys[0], (VOLUMES, C_IN, DEPTH, HEIGHT, WIDTH), 1.0, 6.0, ((0, 2), (2, 128))),
        "conv_one": scatter_about(arg_keys[1], (3, 3, 3, C_IN, C_ONE), (27 * C_IN) ** -0.5, 0.625),
        "bias_one": scatter_about(arg_keys[2], (C_ONE,), 0.5, 3.0, (), jnp.float32),
        "conv_two": scatter_about(arg_keys[3], (3, 3, 3, C_ONE, C_TWO), (27 * C_ONE) ** -0.5, 0.3125),
        "bias_two": scatter_about(arg_keys[4], (C_TWO,), 0.5, 3.0, (), jnp.float32),
        "cotangent": scatter_about(arg_keys[5], (VOLUMES, C_TWO, DEPTH // 2, HEIGHT // 2, WIDTH // 2), (0.125 / (HEIGHT * WIDTH) ** 0.5), 0.008239746, ((0, 2), (2, 128))),
    }


def smooth(values):
    return 0.3 * values + 0.7 * jax.nn.softplus(values)

def slope_of(values):
    return 0.3 + 0.7 * jax.nn.sigmoid(values)

def conv_same(source, kernel):
    return lax.conv_general_dilated(source, kernel, (1, 1, 1), [(1, 1), (1, 1), (1, 1)], dimension_numbers=('NCDHW', 'DHWIO', 'NCDHW'), preferred_element_type=jnp.float32)

def average(values):
    n, c, d, h, w = values.shape
    return values.reshape(n, c, d // 2, 2, h // 2, 2, w // 2, 2).mean(axis=(3, 5, 7))

def spread(values):
    n, c, d, h, w = values.shape
    wide = jnp.broadcast_to(values[:, :, :, None, :, None, :, None], (n, c, d, 2, h, 2, w, 2))
    return wide.reshape(n, c, 2 * d, 2 * h, 2 * w)

def tap_grad(source, upstream):
    n, c, d, h, w = source.shape
    padded = jnp.pad(source[0], ((0, 0), (1, 1), (1, 1), (1, 1)))
    flat_up = upstream[0].reshape(upstream.shape[1], -1)
    pieces = []
    for a in range(3):
        for b in range(3):
            for e in range(3):
                piece = padded[:, a:a + d, b:b + h, e:e + w].reshape(c, -1)
                pieces.append(lax.dot_general(piece, flat_up, (((1,), (1,)), ((), ())), preferred_element_type=jnp.float32))
    return jnp.stack(pieces).reshape(3, 3, 3, c, upstream.shape[1])

def reference(volumes, conv_one, bias_one, conv_two, bias_two, cotangent):

    def one_volume(pair):
        source, upstream = pair
        source = source[None]
        upstream = upstream[None]
        pre_one = conv_same(source, conv_one) + bias_one[None, :, None, None, None]
        pooled = average(smooth(pre_one)).astype(jnp.bfloat16)
        pre_two = conv_same(pooled, conv_two) + bias_two[None, :, None, None, None]
        activations = smooth(pre_two).astype(jnp.bfloat16)
        grad_two = (upstream.astype(jnp.float32) * slope_of(pre_two)).astype(jnp.bfloat16)
        kernel_two = tap_grad(pooled, grad_two)
        bias_grad_two = lax.optimization_barrier(jnp.sum(grad_two.astype(jnp.float32), axis=(0, 2, 3, 4)))
        flipped = jnp.flip(conv_two, (0, 1, 2)).transpose(0, 1, 2, 4, 3)
        grad_pooled = conv_same(grad_two, flipped)
        grad_one = (spread(grad_pooled) * 0.125 * slope_of(pre_one)).astype(jnp.bfloat16)
        kernel_one = tap_grad(source, grad_one)
        bias_grad_one = lax.optimization_barrier(jnp.sum(grad_one.astype(jnp.float32), axis=(0, 2, 3, 4)))
        return (activations[0], kernel_one, bias_grad_one, kernel_two, bias_grad_two)
    results = lax.map(one_volume, (volumes, cotangent))
    return (results[0], lax.optimization_barrier(jnp.sum(results[1], axis=0)), lax.optimization_barrier(jnp.sum(results[2], axis=0)), lax.optimization_barrier(jnp.sum(results[3], axis=0)), lax.optimization_barrier(jnp.sum(results[4], axis=0)))
```

```python
import functools

import jax
import jax.numpy as jnp
from jax import lax
from jax.experimental import pallas as pl
from jax.experimental.pallas import tpu as pltpu
from jax.sharding import Mesh, PartitionSpec as P

BF = jnp.bfloat16
F32 = jnp.float32
ROWS = 16
LANES = 128
CELLS = ROWS * LANES
VMEM_LIMIT = 40 * 1024 * 1024


def iota(shape, dim):
    return lax.broadcasted_iota(jnp.int32, shape, dim)


def dot(a, b, ca=1, cb=0):
    return lax.dot_general(a, b, (((ca,), (cb,)), ((), ())), preferred_element_type=F32)


def flag(mask):
    return jnp.where(mask, 1.0, 0.0).astype(BF)


def smooth(z):
    return 0.3 * z + 0.7 * (jnp.maximum(z, 0.0) + jnp.log(1.0 + jnp.exp(-jnp.abs(z))))


def slope_of(z):
    return 0.65 + 0.35 * jnp.tanh(0.5 * z)


def from_left(x):
    return jnp.where(iota(x.shape, 1) == 0, 0.0, pltpu.roll(x, 1, 1))


def from_right(x):
    return jnp.where(iota(x.shape, 1) == LANES - 1, 0.0, pltpu.roll(x, LANES - 1, 1))


def tile(h):
    return slice(h * LANES, (h + 1) * LANES)


def first_kernel(vol_ref, lo_ref, hi_ref, w_ref, b_ref, patches_ref, slope_ref, pooled_ref):
    cols = iota((256, 512), 1)
    pick_cols = flag(iota((256, 512), 0) == 2 * (cols & 127) + (cols >> 7) - 1)
    rows = iota((256, 128), 0)
    src = iota((256, 128), 1)
    pick_rows = flag(((rows & 3) == (src >> 5)) & ((src & 31) == 2 * (rows >> 4) + ((rows >> 2) & 3) - 1))
    planes = [
        lo_ref[...].reshape(128, 256),
        vol_ref[:, 0].reshape(128, 256),
        vol_ref[:, 1].reshape(128, 256),
        hi_ref[...].reshape(128, 256),
    ]
    for a in range(4):
        wide = dot(planes[a], pick_cols).astype(BF)
        both = dot(pick_rows, wide).astype(BF)
        for e in range(4):
            k = (a * 4 + e) * 16
            for h in range(ROWS):
                patches_ref[k : k + 16, tile(h)] = both[h * 16 : (h + 1) * 16, tile(e)]
    base = w_ref[...]
    weights = jnp.concatenate(
        [
            base if i == 0 else pltpu.roll(base, (i >> 2) * 64 + (i & 1) * 16 + ((i >> 1) & 1) * 4, 1)
            for i in range(8)
        ],
        axis=0,
    ).astype(BF)
    bias = b_ref[...]
    for n in range(8):
        span = slice(n * 256, (n + 1) * 256)
        pre = dot(weights, patches_ref[:, span])
        total = None
        for i in range(8):
            z = pre[i * 16 : (i + 1) * 16] + bias
            slope_ref[i * 16 : (i + 1) * 16, span] = slope_of(z)
            value = smooth(z)
            total = value if total is None else total + value
        pooled_ref[:, span] = (total * 0.125).astype(BF)


def second_kernel(mid_ref, lo_ref, hi_ref, w_ref, b_ref, cot_ref, act_ref, grad_ref, gw_ref, x_ref, g_ref, t_ref, s_ref):
    zero = jnp.zeros((16, LANES), BF)
    for a, ref in enumerate((lo_ref, mid_ref, hi_ref)):
        for b in range(3):
            k = (a * 3 + b) * 16
            for h in range(ROWS):
                q = h + b - 1
                x_ref[k : k + 16, tile(h)] = ref[:, tile(q)] if 0 <= q < ROWS else zero
    x_ref[144:160, :] = jnp.ones((16, CELLS), BF)
    w = w_ref[...].astype(F32)
    weights = jnp.concatenate(
        [
            jnp.concatenate([w[(k * 3 + e) * 16 : (k * 3 + e + 1) * 16] for e in range(3)], axis=1)
            for k in range(9)
        ],
        axis=0,
    )
    weights = jnp.transpose(weights).astype(BF)
    r = iota((512, 512), 0)
    q = iota((512, 512), 1)
    swap = flag(((r >> 5) == (q & 15)) & ((r & 31) == (q >> 4)))
    cot = dot(swap, cot_ref[...].reshape(512, LANES))
    bias = b_ref[...]
    for n in range(4):
        t_ref[...] = dot(weights, x_ref[0:144, n * 512 : (n + 1) * 512])
        for j in range(4):
            h = n * 4 + j
            z = (
                from_left(t_ref[0:32, tile(j)])
                + t_ref[32:64, tile(j)]
                + from_right(t_ref[64:96, tile(j)])
                + bias
            )
            s_ref[h * 32 : (h + 1) * 32] = smooth(z).astype(BF)
            g = (cot[h * 32 : (h + 1) * 32] * slope_of(z)).astype(BF)
            grad_ref[:, tile(h)] = g
            g = g.astype(F32)
            g_ref[0:32, tile(h)] = from_right(g).astype(BF)
            g_ref[32:64, tile(h)] = g.astype(BF)
            g_ref[64:96, tile(h)] = from_left(g).astype(BF)
    g_ref[96:128, :] = jnp.zeros((32, CELLS), BF)
    act_ref[...] = dot(swap, s_ref[...], 0, 0).astype(BF).reshape(32, ROWS, LANES)
    gw_ref[...] = dot(x_ref[...], g_ref[...], 1, 1)


def third_kernel(mid_ref, lo_ref, hi_ref, w_ref, slope_ref, patches_ref, gw_ref, x_ref, t_ref, g_ref):
    for a, ref in enumerate((hi_ref, mid_ref, lo_ref)):
        x_ref[a * 32 : (a + 1) * 32, :] = ref[...]
    w = w_ref[...].astype(F32)
    weights = jnp.concatenate([w[a * 144 : (a + 1) * 144] for a in range(3)], axis=1).astype(BF)
    t_ref[...] = dot(weights, x_ref[...])
    sums = jnp.zeros((16, 1), F32)
    for h in range(ROWS):
        cols = []
        for e in range(3):
            parts = [
                t_ref[(b * 3 + e) * 16 : (b * 3 + e + 1) * 16, tile(h - b + 1)]
                for b in range(3)
                if 0 <= h - b + 1 < ROWS
            ]
            cols.append(functools.reduce(lambda x, y: x + y, parts))
        gp = (from_right(cols[0]) + cols[1] + from_left(cols[2])) * 0.125
        total = None
        for i in range(8):
            g = (gp * slope_ref[i * 16 : (i + 1) * 16, tile(h)]).astype(BF)
            g_ref[i * 16 : (i + 1) * 16, tile(h)] = g
            g = g.astype(F32)
            total = g if total is None else total + g
        sums = sums + jnp.sum(total, axis=1, keepdims=True)
    full = dot(g_ref[...], patches_ref[...], 1, 1)
    acc = full[0:16]
    for i in range(1, 8):
        shift = (i >> 2) * 64 + (i & 1) * 16 + ((i >> 1) & 1) * 4
        acc = acc + pltpu.roll(full[i * 16 : (i + 1) * 16], 256 - shift, 1)
    acc = jnp.where(iota((16, 256), 1) == 255, sums, acc)
    gw_ref[0:16] = acc[:, 0:128]
    gw_ref[16:32] = acc[:, 128:256]


def call(kernel, outs, scratch, name):
    return pl.pallas_call(
        kernel,
        out_shape=outs,
        scratch_shapes=scratch,
        compiler_params=pltpu.CompilerParams(vmem_limit_bytes=VMEM_LIMIT),
        name=name,
    )


def shape(dims, kind):
    return jax.ShapeDtypeStruct(dims, kind)


def halo(head, tail, axis):
    count = lax.axis_size(axis)
    up = [(i, i + 1) for i in range(count - 1)]
    down = [(i + 1, i) for i in range(count - 1)]
    return lax.ppermute(tail, axis, up), lax.ppermute(head, axis, down)


def direct(v, axis):
    n = lax.axis_size(axis)
    for part in [lax.ppermute(v, axis, [(i, (i + k) % n) for i in range(n)]) for k in range(1, n)]:
        v = v + part
    return v


def butterfly(v, axis):
    n = lax.axis_size(axis)
    d = 1
    while d < n:
        v = v + lax.ppermute(v, axis, [(i, i ^ d) for i in range(n)])
        d *= 2
    return v


def body(volumes, conv_one, bias_one, conv_two, bias_two, cotangent):
    depth = ("x", "y", "z")
    vol = volumes[0]
    lo, hi = halo(vol[:, 0], vol[:, 1], depth)
    base = jnp.pad(conv_one.astype(F32).transpose(4, 0, 2, 1, 3), ((0, 0), (0, 1), (0, 1), (0, 1), (0, 0))).reshape(16, 256)
    patches, slopes, pooled = call(
        first_kernel,
        (shape((256, CELLS), BF), shape((128, CELLS), F32), shape((16, CELLS), BF)),
        [],
        "first",
    )(vol, lo, hi, base, bias_one.reshape(16, 1))
    plo, phi = halo(pooled, pooled, depth)
    conv_flat = conv_two.reshape(432, 32)
    act, grad, gw_two = call(
        second_kernel,
        (shape((32, ROWS, LANES), BF), shape((32, CELLS), BF), shape((160, 128), F32)),
        [
            pltpu.VMEM((160, CELLS), BF),
            pltpu.VMEM((128, CELLS), BF),
            pltpu.VMEM((96, 512), F32),
            pltpu.VMEM((512, LANES), BF),
        ],
        "second",
    )(pooled, plo, phi, conv_flat, bias_two.reshape(32, 1), cotangent.reshape(32, ROWS, LANES))
    glo, ghi = halo(grad, grad, depth)
    gw_one = call(
        third_kernel,
        shape((32, 128), F32),
        [pltpu.VMEM((96, CELLS), BF), pltpu.VMEM((144, CELLS), F32), pltpu.VMEM((128, CELLS), BF)],
        "third",
    )(grad, glo, ghi, conv_flat, slopes, patches)
    v = jnp.concatenate([gw_one, gw_two[:152]], axis=0)
    v = direct(direct(direct(v, "core"), "x"), "y")
    v = butterfly(v, "z")
    one = jnp.concatenate([v[0:16], v[16:32]], axis=1).reshape(16, 4, 4, 4, 4)
    grad_conv_one = one[:, :3, :3, :3, :].transpose(1, 3, 2, 4, 0)
    grad_bias_one = one[:, 3, 3, 3, 3]
    grad_conv_two = v[32:176, :96].reshape(3, 3, 16, 3, 32).transpose(0, 1, 3, 2, 4)
    grad_bias_two = v[176, 32:64]
    return act.reshape(1, 32, 1, ROWS, LANES), grad_conv_one, grad_bias_one, grad_conv_two, grad_bias_two


def solution(mesh):
    devices = mesh.devices
    if devices.shape == (2, 128):
        split = (2, 4, 4, 8)
    else:
        split = (2, devices.shape[1], 1, 1)
    fine = Mesh(devices.reshape(split), ("core", "x", "y", "z"))
    cells = P("core", None, ("x", "y", "z"), None, None)
    return jax.shard_map(
        body,
        mesh=fine,
        in_specs=(cells, P(), P(), P(), P(), cells),
        out_specs=(cells, P(), P(), P(), P()),
        check_vma=False,
    )
```

```python
import functools

import jax
import jax.numpy as jnp
from jax import lax
from jax.experimental import pallas as pl
from jax.experimental.pallas import tpu as pltpu
from jax.sharding import Mesh, PartitionSpec as P

BF = jnp.bfloat16
F32 = jnp.float32
ROWS = 16
LANES = 128
CELLS = ROWS * LANES
VMEM_LIMIT = 40 * 1024 * 1024


def iota(shape, dim):
    return lax.broadcasted_iota(jnp.int32, shape, dim)


def dot(a, b, ca=1, cb=0):
    return lax.dot_general(a, b, (((ca,), (cb,)), ((), ())), preferred_element_type=F32)


def flag(mask):
    return jnp.where(mask, 1.0, 0.0).astype(BF)


def smooth(z):
    return 0.3 * z + 0.7 * (jnp.maximum(z, 0.0) + jnp.log(1.0 + jnp.exp(-jnp.abs(z))))


def slope_of(z):
    return 0.65 + 0.35 * jnp.tanh(0.5 * z)


def from_left(x):
    return jnp.where(iota(x.shape, 1) == 0, 0.0, pltpu.roll(x, 1, 1))


def from_right(x):
    return jnp.where(iota(x.shape, 1) == LANES - 1, 0.0, pltpu.roll(x, LANES - 1, 1))


def tile(h):
    return slice(h * LANES, (h + 1) * LANES)


def place(where_ref, even_ref, odd_ref, lo_ref, hi_ref):
    @pl.when(where_ref[0] == 1)
    def _():
        lo_ref[...] = even_ref[...]
        hi_ref[...] = odd_ref[...]

    @pl.when(where_ref[0] == 0)
    def _():
        lo_ref[...] = odd_ref[...]
        hi_ref[...] = even_ref[...]

    @pl.when(where_ref[1] == 1)
    def _():
        lo_ref[...] = jnp.zeros_like(lo_ref)

    @pl.when(where_ref[2] == 1)
    def _():
        hi_ref[...] = jnp.zeros_like(hi_ref)


def first_kernel(
    where_ref, vol_ref, even_ref, odd_ref, w_ref, b_ref, patches_ref, slope_ref, pooled_ref, lo_ref, hi_ref
):
    place(where_ref, even_ref, odd_ref, lo_ref, hi_ref)
    cols = iota((256, 512), 1)
    pick_cols = flag(iota((256, 512), 0) == 2 * (cols & 127) + (cols >> 7) - 1)
    rows = iota((256, 128), 0)
    src = iota((256, 128), 1)
    pick_rows = flag(((rows & 3) == (src >> 5)) & ((src & 31) == 2 * (rows >> 4) + ((rows >> 2) & 3) - 1))
    planes = [
        lo_ref[...].reshape(128, 256),
        vol_ref[:, 0].reshape(128, 256),
        vol_ref[:, 1].reshape(128, 256),
        hi_ref[...].reshape(128, 256),
    ]
    for a in range(4):
        wide = dot(planes[a], pick_cols).astype(BF)
        both = dot(pick_rows, wide).astype(BF)
        for e in range(4):
            k = (a * 4 + e) * 16
            for h in range(ROWS):
                patches_ref[k : k + 16, tile(h)] = both[h * 16 : (h + 1) * 16, tile(e)]
    base = w_ref[...]
    weights = jnp.concatenate(
        [
            base if i == 0 else pltpu.roll(base, (i >> 2) * 64 + (i & 1) * 16 + ((i >> 1) & 1) * 4, 1)
            for i in range(8)
        ],
        axis=0,
    ).astype(BF)
    bias = b_ref[...]
    for n in range(8):
        span = slice(n * 256, (n + 1) * 256)
        pre = dot(weights, patches_ref[:, span])
        total = None
        for i in range(8):
            z = pre[i * 16 : (i + 1) * 16] + bias
            slope_ref[i * 16 : (i + 1) * 16, span] = slope_of(z)
            value = smooth(z)
            total = value if total is None else total + value
        pooled_ref[:, span] = (total * 0.125).astype(BF)


def second_kernel(
    where_ref, mid_ref, even_ref, odd_ref, w_ref, b_ref, cot_ref, act_ref, grad_ref, gw_ref, x_ref, g_ref, t_ref, s_ref, lo_ref, hi_ref
):
    place(where_ref, even_ref, odd_ref, lo_ref, hi_ref)
    zero = jnp.zeros((16, LANES), BF)
    for a, ref in enumerate((lo_ref, mid_ref, hi_ref)):
        for b in range(3):
            k = (a * 3 + b) * 16
            for h in range(ROWS):
                q = h + b - 1
                x_ref[k : k + 16, tile(h)] = ref[:, tile(q)] if 0 <= q < ROWS else zero
    x_ref[144:160, :] = jnp.ones((16, CELLS), BF)
    w = w_ref[...].astype(F32)
    weights = jnp.concatenate(
        [
            jnp.concatenate([w[(k * 3 + e) * 16 : (k * 3 + e + 1) * 16] for e in range(3)], axis=1)
            for k in range(9)
        ],
        axis=0,
    )
    weights = jnp.transpose(weights).astype(BF)
    r = iota((512, 512), 0)
    q = iota((512, 512), 1)
    swap = flag(((r >> 5) == (q & 15)) & ((r & 31) == (q >> 4)))
    cot = dot(swap, cot_ref[...].reshape(512, LANES))
    bias = b_ref[...]
    for n in range(4):
        t_ref[...] = dot(weights, x_ref[0:144, n * 512 : (n + 1) * 512])
        for j in range(4):
            h = n * 4 + j
            z = (
                from_left(t_ref[0:32, tile(j)])
                + t_ref[32:64, tile(j)]
                + from_right(t_ref[64:96, tile(j)])
                + bias
            )
            s_ref[h * 32 : (h + 1) * 32] = smooth(z).astype(BF)
            g = (cot[h * 32 : (h + 1) * 32] * slope_of(z)).astype(BF)
            grad_ref[:, tile(h)] = g
            g = g.astype(F32)
            g_ref[0:32, tile(h)] = from_right(g).astype(BF)
            g_ref[32:64, tile(h)] = g.astype(BF)
            g_ref[64:96, tile(h)] = from_left(g).astype(BF)
    g_ref[96:128, :] = jnp.zeros((32, CELLS), BF)
    act_ref[...] = dot(swap, s_ref[...], 0, 0).astype(BF).reshape(32, ROWS, LANES)
    gw_ref[...] = dot(x_ref[...], g_ref[...], 1, 1)


def third_kernel(where_ref, mid_ref, even_ref, odd_ref, w_ref, slope_ref, patches_ref, gw_ref, x_ref, t_ref, g_ref):
    x_ref[32:64, :] = mid_ref[...]
    place(where_ref, even_ref, odd_ref, x_ref.at[64:96], x_ref.at[0:32])
    w = w_ref[...].astype(F32)
    weights = jnp.concatenate([w[a * 144 : (a + 1) * 144] for a in range(3)], axis=1).astype(BF)
    t_ref[...] = dot(weights, x_ref[...])
    sums = jnp.zeros((16, 1), F32)
    for h in range(ROWS):
        cols = []
        for e in range(3):
            parts = [
                t_ref[(b * 3 + e) * 16 : (b * 3 + e + 1) * 16, tile(h - b + 1)]
                for b in range(3)
                if 0 <= h - b + 1 < ROWS
            ]
            cols.append(functools.reduce(lambda x, y: x + y, parts))
        gp = (from_right(cols[0]) + cols[1] + from_left(cols[2])) * 0.125
        total = None
        for i in range(8):
            g = (gp * slope_ref[i * 16 : (i + 1) * 16, tile(h)]).astype(BF)
            g_ref[i * 16 : (i + 1) * 16, tile(h)] = g
            g = g.astype(F32)
            total = g if total is None else total + g
        sums = sums + jnp.sum(total, axis=1, keepdims=True)
    full = dot(g_ref[...], patches_ref[...], 1, 1)
    acc = full[0:16]
    for i in range(1, 8):
        shift = (i >> 2) * 64 + (i & 1) * 16 + ((i >> 1) & 1) * 4
        acc = acc + pltpu.roll(full[i * 16 : (i + 1) * 16], 256 - shift, 1)
    acc = jnp.where(iota((16, 256), 1) == 255, sums, acc)
    gw_ref[0:16] = acc[:, 0:128]
    gw_ref[16:32] = acc[:, 128:256]


def last_kernel(mine_ref, other_ref, one_ref, bias_one_ref, two_ref, bias_two_ref):
    v = mine_ref[...] + other_ref[...]
    turned = jnp.transpose(jnp.concatenate([v[0:16], v[16:32]], axis=1))
    for a in range(3):
        for b in range(3):
            k = a * 3 + b
            for e in range(3):
                row = a * 64 + e * 16 + b * 4
                one_ref[k * 3 + e] = turned[row : row + 4]
                two_ref[k * 3 + e] = v[32 + k * 16 : 48 + k * 16, e * 32 : (e + 1) * 32]
    bias_one_ref[...] = turned[255:256]
    bias_two_ref[...] = v[176:177, 32:64]


def call(kernel, outs, scratch, name, where=True):
    count = {"first": 6, "second": 7, "third": 7, "last": 2}[name]
    vmem = pl.BlockSpec(memory_space=pltpu.VMEM)
    specs = [pl.BlockSpec(memory_space=pltpu.SMEM) if where and i == 0 else vmem for i in range(count)]
    return pl.pallas_call(
        kernel,
        out_shape=outs,
        in_specs=specs,
        scratch_shapes=scratch,
        compiler_params=pltpu.CompilerParams(vmem_limit_bytes=VMEM_LIMIT),
        name=name,
    )


def shape(dims, kind):
    return jax.ShapeDtypeStruct(dims, kind)


def pairs(even, odd, axis):
    n = lax.axis_size(axis)
    first = lax.ppermute(even, axis, [(i, i ^ 1) for i in range(n)])
    second = lax.ppermute(odd, axis, [(i, (((i + 1) ^ 1) - 1) % n) for i in range(n)])
    return first, second


def body(volumes, conv_one, bias_one, conv_two, bias_two, cotangent):
    depth = ("x", "y", "z")
    vol = volumes[0]
    place_at = lax.axis_index(depth)
    odd = place_at % 2
    where = jnp.stack([odd, place_at == 0, place_at == lax.axis_size(depth) - 1]).astype(jnp.int32)
    head, tail = vol[:, 0], vol[:, 1]
    even_part, odd_part = pairs(jnp.where(odd == 1, head, tail), jnp.where(odd == 1, tail, head), depth)
    base = jnp.pad(conv_one.astype(F32).transpose(4, 0, 2, 1, 3), ((0, 0), (0, 1), (0, 1), (0, 1), (0, 0))).reshape(16, 256)
    plane = pltpu.VMEM((4, 32, 256), BF)
    patches, slopes, pooled = call(
        first_kernel,
        (shape((256, CELLS), BF), shape((128, CELLS), F32), shape((16, CELLS), BF)),
        [plane, plane],
        "first",
    )(where, vol, even_part, odd_part, base, bias_one.reshape(16, 1))
    even_part, odd_part = pairs(pooled, pooled, depth)
    conv_flat = conv_two.reshape(432, 32)
    act, grad, gw_two = call(
        second_kernel,
        (shape((32, ROWS, LANES), BF), shape((32, CELLS), BF), shape((160, 128), F32)),
        [
            pltpu.VMEM((160, CELLS), BF),
            pltpu.VMEM((128, CELLS), BF),
            pltpu.VMEM((96, 512), F32),
            pltpu.VMEM((512, LANES), BF),
            pltpu.VMEM((16, CELLS), BF),
            pltpu.VMEM((16, CELLS), BF),
        ],
        "second",
    )(where, pooled, even_part, odd_part, conv_flat, bias_two.reshape(32, 1), cotangent.reshape(32, ROWS, LANES))
    even_part, odd_part = pairs(grad, grad, depth)
    gw_one = call(
        third_kernel,
        shape((32, 128), F32),
        [pltpu.VMEM((96, CELLS), BF), pltpu.VMEM((144, CELLS), F32), pltpu.VMEM((128, CELLS), BF)],
        "third",
    )(where, grad, even_part, odd_part, conv_flat, slopes, patches)
    v = jnp.concatenate([gw_one, gw_two[:152]], axis=0)
    n = {axis: lax.axis_size(axis) for axis in ("z", "y", "x", "core")}
    steps = [
        (axis, [(i, i ^ 2 if d == 4 and size == 8 else i ^ (d - 1)) for i in range(size)])
        for axis, size in n.items()
        for d in (2, 4, 8)
        if d <= size
    ]
    for axis, perm in steps[:-1]:
        v = v + lax.ppermute(v, axis, perm)
    one, sum_one, two, sum_two = call(
        last_kernel,
        (shape((27, 4, 16), F32), shape((1, 16), F32), shape((27, 16, 32), F32), shape((1, 32), F32)),
        [],
        "last",
        where=False,
    )(v, lax.ppermute(v, *steps[-1]))
    return (
        act.reshape(1, 32, 1, ROWS, LANES),
        one.reshape(3, 3, 3, 4, 16),
        sum_one.reshape(16),
        two.reshape(3, 3, 3, 16, 32),
        sum_two.reshape(32),
    )


def solution(mesh):
    devices = mesh.devices
    if devices.shape == (2, 128):
        split = (2, 4, 4, 8)
    else:
        split = (2, 1, 1, devices.shape[1])
    fine = Mesh(devices.reshape(split), ("core", "x", "y", "z"))
    cells = P("core", None, ("x", "y", "z"), None, None)
    return jax.shard_map(
        body,
        mesh=fine,
        in_specs=(cells, P(), P(), P(), P(), cells),
        out_specs=(cells, P(), P(), P(), P()),
        check_vma=False,
    )
```

```python
import functools

import jax
import jax.numpy as jnp
from jax import lax
from jax.experimental import pallas as pl
from jax.experimental.pallas import tpu as pltpu
from jax.sharding import Mesh, PartitionSpec as P

BF = jnp.bfloat16
F32 = jnp.float32
ROWS = 16
LANES = 128
CELLS = ROWS * LANES
VMEM_LIMIT = 40 * 1024 * 1024


def iota(shape, dim):
    return lax.broadcasted_iota(jnp.int32, shape, dim)


def dot(a, b, ca=1, cb=0):
    return lax.dot_general(a, b, (((ca,), (cb,)), ((), ())), preferred_element_type=F32)


def flag(mask):
    return jnp.where(mask, 1.0, 0.0).astype(BF)


def smooth(z):
    return 0.3 * z + 0.7 * (jnp.maximum(z, 0.0) + jnp.log(1.0 + jnp.exp(-jnp.abs(z))))


def slope_of(z):
    return 0.65 + 0.35 * jnp.tanh(0.5 * z)


def from_left(x):
    return jnp.where(iota(x.shape, 1) == 0, 0.0, pltpu.roll(x, 1, 1))


def from_right(x):
    return jnp.where(iota(x.shape, 1) == LANES - 1, 0.0, pltpu.roll(x, LANES - 1, 1))


def tile(h):
    return slice(h * LANES, (h + 1) * LANES)


def spot():
    at = (lax.axis_index("x") * lax.axis_size("y") + lax.axis_index("y")) * lax.axis_size("z") + lax.axis_index("z")
    return at, lax.axis_size("x") * lax.axis_size("y") * lax.axis_size("z")


def place(even_ref, odd_ref, lo_ref, hi_ref):
    at, count = spot()

    @pl.when(lax.rem(at, 2) == 1)
    def _():
        lo_ref[...] = even_ref[...]
        hi_ref[...] = odd_ref[...]

    @pl.when(lax.rem(at, 2) == 0)
    def _():
        lo_ref[...] = odd_ref[...]
        hi_ref[...] = even_ref[...]

    @pl.when(at == 0)
    def _():
        lo_ref[...] = jnp.zeros_like(lo_ref)

    @pl.when(at == count - 1)
    def _():
        hi_ref[...] = jnp.zeros_like(hi_ref)


def first_kernel(
    vol_ref, even_ref, odd_ref, w_ref, b_ref, patches_ref, slope_ref, pooled_ref, lo_ref, hi_ref
):
    place(even_ref, odd_ref, lo_ref, hi_ref)
    cols = iota((256, 512), 1)
    pick_cols = flag(iota((256, 512), 0) == 2 * (cols & 127) + (cols >> 7) - 1)
    rows = iota((256, 128), 0)
    src = iota((256, 128), 1)
    pick_rows = flag(((rows & 3) == (src >> 5)) & ((src & 31) == 2 * (rows >> 4) + ((rows >> 2) & 3) - 1))
    planes = [
        lo_ref[...].reshape(128, 256),
        vol_ref[:, 0].reshape(128, 256),
        vol_ref[:, 1].reshape(128, 256),
        hi_ref[...].reshape(128, 256),
    ]
    for a in range(4):
        wide = dot(planes[a], pick_cols).astype(BF)
        both = dot(pick_rows, wide).astype(BF)
        for e in range(4):
            k = (a * 4 + e) * 16
            for h in range(ROWS):
                patches_ref[k : k + 16, tile(h)] = both[h * 16 : (h + 1) * 16, tile(e)]
    base = w_ref[...]
    weights = jnp.concatenate(
        [
            base if i == 0 else pltpu.roll(base, (i >> 2) * 64 + (i & 1) * 16 + ((i >> 1) & 1) * 4, 1)
            for i in range(8)
        ],
        axis=0,
    ).astype(BF)
    bias = b_ref[...]
    for n in range(8):
        span = slice(n * 256, (n + 1) * 256)
        pre = dot(weights, patches_ref[:, span])
        total = None
        for i in range(8):
            z = pre[i * 16 : (i + 1) * 16] + bias
            slope_ref[i * 16 : (i + 1) * 16, span] = slope_of(z)
            value = smooth(z)
            total = value if total is None else total + value
        pooled_ref[:, span] = (total * 0.125).astype(BF)


def second_kernel(
    mid_ref, even_ref, odd_ref, w_ref, b_ref, cot_ref, act_ref, grad_ref, gw_ref, x_ref, g_ref, t_ref, s_ref, lo_ref, hi_ref
):
    place(even_ref, odd_ref, lo_ref, hi_ref)
    zero = jnp.zeros((16, LANES), BF)
    for a, ref in enumerate((lo_ref, mid_ref, hi_ref)):
        for b in range(3):
            k = (a * 3 + b) * 16
            for h in range(ROWS):
                q = h + b - 1
                x_ref[k : k + 16, tile(h)] = ref[:, tile(q)] if 0 <= q < ROWS else zero
    x_ref[144:160, :] = jnp.ones((16, CELLS), BF)
    w = w_ref[...].astype(F32)
    weights = jnp.concatenate(
        [
            jnp.concatenate([w[(k * 3 + e) * 16 : (k * 3 + e + 1) * 16] for e in range(3)], axis=1)
            for k in range(9)
        ],
        axis=0,
    )
    weights = jnp.transpose(weights).astype(BF)
    r = iota((512, 512), 0)
    q = iota((512, 512), 1)
    swap = flag(((r >> 5) == (q & 15)) & ((r & 31) == (q >> 4)))
    cot = dot(swap, cot_ref[...].reshape(512, LANES))
    bias = b_ref[...]
    for n in range(4):
        t_ref[...] = dot(weights, x_ref[0:144, n * 512 : (n + 1) * 512])
        for j in range(4):
            h = n * 4 + j
            z = (
                from_left(t_ref[0:32, tile(j)])
                + t_ref[32:64, tile(j)]
                + from_right(t_ref[64:96, tile(j)])
                + bias
            )
            s_ref[h * 32 : (h + 1) * 32] = smooth(z).astype(BF)
            g = (cot[h * 32 : (h + 1) * 32] * slope_of(z)).astype(BF)
            grad_ref[:, tile(h)] = g
            g = g.astype(F32)
            g_ref[0:32, tile(h)] = from_right(g).astype(BF)
            g_ref[32:64, tile(h)] = g.astype(BF)
            g_ref[64:96, tile(h)] = from_left(g).astype(BF)
    g_ref[96:128, :] = jnp.zeros((32, CELLS), BF)
    act_ref[...] = dot(swap, s_ref[...], 0, 0).astype(BF).reshape(32, ROWS, LANES)
    gw_ref[...] = dot(x_ref[...], g_ref[...], 1, 1)


def third_kernel(mid_ref, even_ref, odd_ref, w_ref, slope_ref, patches_ref, gw_two_ref, gw_ref, x_ref, t_ref, g_ref):
    x_ref[32:64, :] = mid_ref[...]
    place(even_ref, odd_ref, x_ref.at[64:96], x_ref.at[0:32])
    w = w_ref[...].astype(F32)
    weights = jnp.concatenate([w[a * 144 : (a + 1) * 144] for a in range(3)], axis=1).astype(BF)
    t_ref[...] = dot(weights, x_ref[...])
    sums = jnp.zeros((16, 1), F32)
    for h in range(ROWS):
        cols = []
        for e in range(3):
            parts = [
                t_ref[(b * 3 + e) * 16 : (b * 3 + e + 1) * 16, tile(h - b + 1)]
                for b in range(3)
                if 0 <= h - b + 1 < ROWS
            ]
            cols.append(functools.reduce(lambda x, y: x + y, parts))
        gp = (from_right(cols[0]) + cols[1] + from_left(cols[2])) * 0.125
        total = None
        for i in range(8):
            g = (gp * slope_ref[i * 16 : (i + 1) * 16, tile(h)]).astype(BF)
            g_ref[i * 16 : (i + 1) * 16, tile(h)] = g
            g = g.astype(F32)
            total = g if total is None else total + g
        sums = sums + jnp.sum(total, axis=1, keepdims=True)
    full = dot(g_ref[...], patches_ref[...], 1, 1)
    acc = full[0:16]
    for i in range(1, 8):
        shift = (i >> 2) * 64 + (i & 1) * 16 + ((i >> 1) & 1) * 4
        acc = acc + pltpu.roll(full[i * 16 : (i + 1) * 16], 256 - shift, 1)
    acc = jnp.where(iota((16, 256), 1) == 255, sums, acc)
    gw_ref[...] = gw_two_ref[...]
    for i in range(8):
        gw_ref[i * 16 : (i + 1) * 16, 96:128] = acc[:, i * 32 : (i + 1) * 32]


def last_kernel(mine_ref, other_ref, one_ref, bias_one_ref, two_ref, bias_two_ref):
    mine = mine_ref[...]
    other = other_ref[...]
    low = lax.axis_index("core") == 0
    v = jnp.concatenate([jnp.where(low, mine, other), jnp.where(low, other, mine)], axis=0)
    turned = jnp.transpose(jnp.concatenate([v[i * 16 : (i + 1) * 16, 96:128] for i in range(8)], axis=1))
    for a in range(3):
        for b in range(3):
            k = a * 3 + b
            for e in range(3):
                row = a * 64 + e * 16 + b * 4
                one_ref[k * 3 + e] = turned[row : row + 4]
                two_ref[k * 3 + e] = v[k * 16 : (k + 1) * 16, e * 32 : (e + 1) * 32]
    bias_one_ref[...] = turned[255:256]
    bias_two_ref[...] = v[144:145, 32:64]


def call(kernel, outs, scratch, name):
    return pl.pallas_call(
        kernel,
        out_shape=outs,
        scratch_shapes=scratch,
        compiler_params=pltpu.CompilerParams(vmem_limit_bytes=VMEM_LIMIT),
        name=name,
    )


def shape(dims, kind):
    return jax.ShapeDtypeStruct(dims, kind)


def pairs(even, odd, axis):
    n = lax.axis_size(axis)
    first = lax.ppermute(even, axis, [(i, i ^ 1) for i in range(n)])
    second = lax.ppermute(odd, axis, [(i, (((i + 1) ^ 1) - 1) % n) for i in range(n)])
    return first, second


def body(volumes, conv_one, bias_one, conv_two, bias_two, cotangent):
    depth = ("x", "y", "z")
    vol = volumes[0]
    place_at = lax.axis_index(depth)
    odd = place_at % 2
    head, tail = vol[:, 0], vol[:, 1]
    even_part, odd_part = pairs(jnp.where(odd == 1, head, tail), jnp.where(odd == 1, tail, head), depth)
    base = jnp.pad(conv_one.astype(F32).transpose(4, 0, 2, 1, 3), ((0, 0), (0, 1), (0, 1), (0, 1), (0, 0))).reshape(16, 256)
    plane = pltpu.VMEM((4, 32, 256), BF)
    patches, slopes, pooled = call(
        first_kernel,
        (shape((256, CELLS), BF), shape((128, CELLS), F32), shape((16, CELLS), BF)),
        [plane, plane],
        "first",
    )(vol, even_part, odd_part, base, bias_one.reshape(16, 1))
    even_part, odd_part = pairs(pooled, pooled, depth)
    conv_flat = conv_two.reshape(432, 32)
    act, grad, gw_two = call(
        second_kernel,
        (shape((32, ROWS, LANES), BF), shape((32, CELLS), BF), shape((160, 128), F32)),
        [
            pltpu.VMEM((160, CELLS), BF),
            pltpu.VMEM((128, CELLS), BF),
            pltpu.VMEM((96, 512), F32),
            pltpu.VMEM((512, LANES), BF),
            pltpu.VMEM((16, CELLS), BF),
            pltpu.VMEM((16, CELLS), BF),
        ],
        "second",
    )(pooled, even_part, odd_part, conv_flat, bias_two.reshape(32, 1), cotangent.reshape(32, ROWS, LANES))
    even_part, odd_part = pairs(grad, grad, depth)
    v = call(
        third_kernel,
        shape((160, 128), F32),
        [pltpu.VMEM((96, CELLS), BF), pltpu.VMEM((144, CELLS), F32), pltpu.VMEM((128, CELLS), BF)],
        "third",
    )(grad, even_part, odd_part, conv_flat, slopes, patches, gw_two)
    low = lax.axis_index("core") == 0
    swap = [(0, 1), (1, 0)]
    v = jnp.where(low, v[:80], v[80:]) + lax.ppermute(jnp.where(low, v[80:], v[:80]), "core", swap)
    n = {axis: lax.axis_size(axis) for axis in ("z", "y", "x")}
    steps = [
        (axis, [(i, i ^ 2 if d == 4 and size == 8 else i ^ (d - 1)) for i in range(size)])
        for axis, size in n.items()
        for d in (2, 4, 8)
        if d <= size
    ]
    for axis, perm in steps:
        v = v + lax.ppermute(v, axis, perm)
    one, sum_one, two, sum_two = call(
        last_kernel,
        (shape((27, 4, 16), F32), shape((1, 16), F32), shape((27, 16, 32), F32), shape((1, 32), F32)),
        [],
        "last",
    )(v, lax.ppermute(v, "core", swap))
    return (
        act.reshape(1, 32, 1, ROWS, LANES),
        one.reshape(3, 3, 3, 4, 16),
        sum_one.reshape(16),
        two.reshape(3, 3, 3, 16, 32),
        sum_two.reshape(32),
    )


def solution(mesh):
    devices = mesh.devices
    if devices.shape == (2, 128):
        split = (2, 4, 4, 8)
    else:
        split = (2, 1, 1, devices.shape[1])
    fine = Mesh(devices.reshape(split), ("core", "x", "y", "z"))
    cells = P("core", None, ("x", "y", "z"), None, None)
    return jax.shard_map(
        body,
        mesh=fine,
        in_specs=(cells, P(), P(), P(), P(), cells),
        out_specs=(cells, P(), P(), P(), P()),
        check_vma=False,
    )
```

```python
import functools

import jax
import jax.numpy as jnp
from jax import lax
from jax.experimental import pallas as pl
from jax.experimental.pallas import tpu as pltpu
from jax.sharding import Mesh, PartitionSpec as P

BF = jnp.bfloat16
F32 = jnp.float32
ROWS = 16
LANES = 128
CELLS = ROWS * LANES
GROUPS = ((1, 32), (8, 96), (24, 2), (7,))
VMEM_LIMIT = 40 * 1024 * 1024


def iota(shape, dim):
    return lax.broadcasted_iota(jnp.int32, shape, dim)


def dot(a, b, ca=1, cb=0):
    return lax.dot_general(a, b, (((ca,), (cb,)), ((), ())), preferred_element_type=F32)


def flag(mask):
    return jnp.where(mask, 1.0, 0.0).astype(BF)


def smooth(z):
    return 0.3 * z + 0.7 * (jnp.maximum(z, 0.0) + jnp.log(1.0 + jnp.exp(-jnp.abs(z))))


def slope_of(z):
    return 0.65 + 0.35 * jnp.tanh(0.5 * z)


def from_left(x):
    return jnp.where(iota(x.shape, 1) == 0, 0.0, pltpu.roll(x, 1, 1))


def from_right(x):
    return jnp.where(iota(x.shape, 1) == LANES - 1, 0.0, pltpu.roll(x, LANES - 1, 1))


def tile(h):
    return slice(h * LANES, (h + 1) * LANES)


def spot():
    at = (lax.axis_index("x") * lax.axis_size("y") + lax.axis_index("y")) * lax.axis_size("z") + lax.axis_index("z")
    return at, lax.axis_size("x") * lax.axis_size("y") * lax.axis_size("z")


def place(even_ref, odd_ref, lo_ref, hi_ref, step=1):
    at, count = spot()
    upper = lax.rem(at // step, 2) == 1

    @pl.when(upper)
    def _():
        lo_ref[...] = even_ref[...]
        hi_ref[...] = odd_ref[...]

    @pl.when(jnp.logical_not(upper))
    def _():
        lo_ref[...] = odd_ref[...]
        hi_ref[...] = even_ref[...]

    @pl.when(at < step)
    def _():
        lo_ref[...] = jnp.zeros_like(lo_ref)

    @pl.when(at >= count - step)
    def _():
        hi_ref[...] = jnp.zeros_like(hi_ref)


def pack_kernel(vol_ref, cot_ref, even_ref, odd_ref):
    cot = cot_ref[...].reshape(512, LANES)
    even_ref[0:512] = cot
    odd_ref[0:512] = cot
    at, _ = spot()
    upper = lax.rem(at, 2) == 1

    def put(even, odd):
        for ref, d in ((even_ref, even), (odd_ref, odd)):
            plane = vol_ref[:, d].reshape(128, 256)
            ref[512:640] = plane[:, 0:128]
            ref[640:768] = plane[:, 128:256]

    @pl.when(upper)
    def _():
        put(0, 1)

    @pl.when(jnp.logical_not(upper))
    def _():
        put(1, 0)


def first_kernel(
    vol_ref, even_ref, odd_ref, w_ref, b_ref, patches_ref, slope_ref, pooled_ref, lo_ref, hi_ref
):
    place(even_ref.at[512:768], odd_ref.at[512:768], lo_ref, hi_ref)
    cols = iota((256, 512), 1)
    pick_cols = flag(iota((256, 512), 0) == 2 * (cols & 127) + (cols >> 7) - 1)
    rows = iota((256, 128), 0)
    src = iota((256, 128), 1)
    pick_rows = flag(((rows & 3) == (src >> 5)) & ((src & 31) == 2 * (rows >> 4) + ((rows >> 2) & 3) - 1))
    planes = [
        jnp.concatenate([lo_ref[0:128], lo_ref[128:256]], axis=1),
        vol_ref[:, 0].reshape(128, 256),
        vol_ref[:, 1].reshape(128, 256),
        jnp.concatenate([hi_ref[0:128], hi_ref[128:256]], axis=1),
    ]
    for a in range(4):
        wide = dot(planes[a], pick_cols).astype(BF)
        both = dot(pick_rows, wide).astype(BF)
        for e in range(4):
            k = (a * 4 + e) * 16
            for h in range(ROWS):
                patches_ref[k : k + 16, tile(h)] = both[h * 16 : (h + 1) * 16, tile(e)]
    base = w_ref[...]
    weights = jnp.concatenate(
        [
            base if i == 0 else pltpu.roll(base, (i >> 2) * 64 + (i & 1) * 16 + ((i >> 1) & 1) * 4, 1)
            for i in range(8)
        ],
        axis=0,
    ).astype(BF)
    bias = b_ref[...]
    for n in range(8):
        span = slice(n * 256, (n + 1) * 256)
        pre = dot(weights, patches_ref[:, span])
        total = None
        for i in range(8):
            z = pre[i * 16 : (i + 1) * 16] + bias
            slope_ref[i * 16 : (i + 1) * 16, span] = slope_of(z)
            value = smooth(z)
            total = value if total is None else total + value
        pooled_ref[:, span] = (total * 0.125).astype(BF)


def second_kernel(
    mid_ref, near_even_ref, near_odd_ref, far_even_ref, far_odd_ref, w_ref, b_ref, cot_ref, cot_even_ref, cot_odd_ref,
    slope_ref, patches_ref, act_ref, gw_ref, p_ref, x_ref, g_ref, t_ref, s_ref, cot_lo_ref, cot_hi_ref, u_ref, up_ref, one_ref
):
    place(near_even_ref, near_odd_ref, p_ref.at[16:32], p_ref.at[48:64])
    place(far_even_ref, far_odd_ref, p_ref.at[0:16], p_ref.at[64:80], 2)
    p_ref[32:48, :] = mid_ref[...]
    place(cot_even_ref.at[0:512], cot_odd_ref.at[0:512], cot_lo_ref, cot_hi_ref)
    zero = jnp.zeros((16, LANES), BF)
    for a in range(5):
        for b in range(3):
            k = (a * 3 + b) * 16
            for h in range(ROWS):
                q = h + b - 1
                x_ref[k : k + 16, tile(h)] = p_ref[a * 16 : (a + 1) * 16, tile(q)] if 0 <= q < ROWS else zero
    w = w_ref[...].astype(F32)
    weights = jnp.concatenate(
        [
            jnp.concatenate([w[(k * 3 + e) * 16 : (k * 3 + e + 1) * 16] for e in range(3)], axis=1)
            for k in range(9)
        ],
        axis=0,
    )
    weights = jnp.transpose(weights).astype(BF)
    r = iota((512, 512), 0)
    q = iota((512, 512), 1)
    swap = flag(((r >> 5) == (q & 15)) & ((r & 31) == (q >> 4)))
    cots = jnp.concatenate([c[...].reshape(512, LANES) for c in (cot_lo_ref, cot_ref, cot_hi_ref)], axis=1)
    cots = dot(swap, cots)
    bias = b_ref[...]
    for d in range(3):
        for n in range(4):
            t_ref[...] = dot(weights, x_ref[d * 48 : d * 48 + 144, n * 512 : (n + 1) * 512])
            for j in range(4):
                h = n * 4 + j
                z = (
                    from_left(t_ref[0:32, tile(j)])
                    + t_ref[32:64, tile(j)]
                    + from_right(t_ref[64:96, tile(j)])
                    + bias
                )
                g = (cots[h * 32 : (h + 1) * 32, tile(d)] * slope_of(z)).astype(BF)
                up_ref[(2 - d) * 32 : (3 - d) * 32, tile(h)] = g
                if d == 1:
                    s_ref[h * 32 : (h + 1) * 32] = smooth(z).astype(BF)
                    g = g.astype(F32)
                    g_ref[0:32, tile(h)] = from_right(g).astype(BF)
                    g_ref[32:64, tile(h)] = g.astype(BF)
                    g_ref[64:96, tile(h)] = from_left(g).astype(BF)
    g_ref[96:128, :] = jnp.zeros((32, CELLS), BF)
    act_ref[...] = dot(swap, s_ref[...], 0, 0).astype(BF).reshape(32, ROWS, LANES)
    gw_ref[0:144] = dot(x_ref[48:192], g_ref[...], 1, 1)
    gw_ref[144:160] = dot(jnp.ones((16, CELLS), BF), g_ref[...], 1, 1)
    weights = jnp.concatenate([w[a * 144 : (a + 1) * 144] for a in range(3)], axis=1).astype(BF)
    u_ref[...] = dot(weights, up_ref[...])
    sums = jnp.zeros((16, 1), F32)
    for h in range(ROWS):
        cols = []
        for e in range(3):
            parts = [
                u_ref[(b * 3 + e) * 16 : (b * 3 + e + 1) * 16, tile(h - b + 1)]
                for b in range(3)
                if 0 <= h - b + 1 < ROWS
            ]
            cols.append(functools.reduce(lambda x, y: x + y, parts))
        gp = (from_right(cols[0]) + cols[1] + from_left(cols[2])) * 0.125
        total = None
        for i in range(8):
            g = (gp * slope_ref[i * 16 : (i + 1) * 16, tile(h)]).astype(BF)
            one_ref[i * 16 : (i + 1) * 16, tile(h)] = g
            g = g.astype(F32)
            total = g if total is None else total + g
        sums = sums + jnp.sum(total, axis=1, keepdims=True)
    full = dot(one_ref[...], patches_ref[...], 1, 1)
    acc = full[0:16]
    for i in range(1, 8):
        shift = (i >> 2) * 64 + (i & 1) * 16 + ((i >> 1) & 1) * 4
        acc = acc + pltpu.roll(full[i * 16 : (i + 1) * 16], 256 - shift, 1)
    acc = jnp.where(iota((16, 256), 1) == 255, sums, acc)
    for i in range(8):
        gw_ref[i * 16 : (i + 1) * 16, 96:128] = acc[:, i * 32 : (i + 1) * 32]


def last_kernel(mine_ref, other_ref, one_ref, bias_one_ref, two_ref, bias_two_ref):
    mine = mine_ref[...]
    other = other_ref[...]
    low = lax.axis_index("core") == 0
    v = jnp.concatenate([jnp.where(low, mine, other), jnp.where(low, other, mine)], axis=0)
    turned = jnp.transpose(jnp.concatenate([v[i * 16 : (i + 1) * 16, 96:128] for i in range(8)], axis=1))
    for a in range(3):
        for b in range(3):
            k = a * 3 + b
            for e in range(3):
                row = a * 64 + e * 16 + b * 4
                one_ref[k * 3 + e] = turned[row : row + 4]
                two_ref[k * 3 + e] = v[k * 16 : (k + 1) * 16, e * 32 : (e + 1) * 32]
    bias_one_ref[...] = turned[255:256]
    bias_two_ref[...] = v[144:145, 32:64]


def call(kernel, outs, scratch, name):
    return pl.pallas_call(
        kernel,
        out_shape=outs,
        scratch_shapes=scratch,
        compiler_params=pltpu.CompilerParams(vmem_limit_bytes=VMEM_LIMIT),
        name=name,
    )


def shape(dims, kind):
    return jax.ShapeDtypeStruct(dims, kind)


def pairs(even, odd, axis, step=1):
    n = lax.axis_size(axis)
    first = lax.ppermute(even, axis, [(i, i ^ step) for i in range(n)])
    second = lax.ppermute(odd, axis, [(i, (((i + step) ^ step) - step) % n) for i in range(n)])
    return first, second


def group_sum(v, axis, masks):
    n = lax.axis_size(axis)
    places = [0]
    for m in masks:
        places = places + [p ^ m for p in places]
    parts = [v if p == 0 else lax.ppermute(v, axis, [(i, i ^ p) for i in range(n)]) for p in places]
    while len(parts) > 1:
        half = len(parts) // 2
        parts = [parts[i] + parts[i + half] for i in range(half)]
    return parts[0]


def body(volumes, conv_one, bias_one, conv_two, bias_two, cotangent):
    depth = ("x", "y", "z")
    vol = volumes[0]
    cot = cotangent.reshape(32, ROWS, LANES)
    packed = shape((768, LANES), BF)
    even_part, odd_part = pairs(*call(pack_kernel, (packed, packed), [], "pack")(vol, cot), depth)
    base = jnp.pad(conv_one.astype(F32).transpose(4, 0, 2, 1, 3), ((0, 0), (0, 1), (0, 1), (0, 1), (0, 0))).reshape(16, 256)
    plane = pltpu.VMEM((256, LANES), BF)
    patches, slopes, pooled = call(
        first_kernel,
        (shape((256, CELLS), BF), shape((128, CELLS), F32), shape((16, CELLS), BF)),
        [plane, plane],
        "first",
    )(vol, even_part, odd_part, base, bias_one.reshape(16, 1))
    near = pairs(pooled, pooled, depth)
    far = pairs(pooled, pooled, depth, 2)
    act, v = call(
        second_kernel,
        (shape((32, ROWS, LANES), BF), shape((160, 128), F32)),
        [
            pltpu.VMEM((80, CELLS), BF),
            pltpu.VMEM((240, CELLS), BF),
            pltpu.VMEM((128, CELLS), BF),
            pltpu.VMEM((96, 512), F32),
            pltpu.VMEM((512, LANES), BF),
            pltpu.VMEM((512, LANES), BF),
            pltpu.VMEM((512, LANES), BF),
            pltpu.VMEM((144, CELLS), F32),
            pltpu.VMEM((96, CELLS), BF),
            pltpu.VMEM((128, CELLS), BF),
        ],
        "second",
    )(pooled, *near, *far, conv_two.reshape(432, 32), bias_two.reshape(32, 1), cot, even_part, odd_part, slopes, patches)
    low = lax.axis_index("core") == 0
    swap = [(0, 1), (1, 0)]
    v = jnp.where(low, v[:80], v[80:]) + lax.ppermute(jnp.where(low, v[80:], v[:80]), "core", swap)
    for masks in GROUPS if lax.axis_size(depth) == 128 else ((1, 2), (7,)):
        v = group_sum(v, depth, masks)
    one, sum_one, two, sum_two = call(
        last_kernel,
        (shape((27, 4, 16), F32), shape((1, 16), F32), shape((27, 16, 32), F32), shape((1, 32), F32)),
        [],
        "last",
    )(v, lax.ppermute(v, "core", swap))
    return (
        act.reshape(1, 32, 1, ROWS, LANES),
        one.reshape(3, 3, 3, 4, 16),
        sum_one.reshape(16),
        two.reshape(3, 3, 3, 16, 32),
        sum_two.reshape(32),
    )


def solution(mesh):
    devices = mesh.devices
    if devices.shape == (2, 128):
        split = (2, 4, 4, 8)
    else:
        split = (2, 1, 1, devices.shape[1])
    fine = Mesh(devices.reshape(split), ("core", "x", "y", "z"))
    cells = P("core", None, ("x", "y", "z"), None, None)
    return jax.shard_map(
        body,
        mesh=fine,
        in_specs=(cells, P(), P(), P(), P(), cells),
        out_specs=(cells, P(), P(), P(), P()),
        check_vma=False,
    )
```

```python
import functools

import jax
import jax.numpy as jnp
from jax import lax
from jax.experimental import pallas as pl
from jax.experimental.pallas import tpu as pltpu
from jax.sharding import Mesh, PartitionSpec as P

BF = jnp.bfloat16
F32 = jnp.float32
ROWS = 16
LANES = 128
CELLS = ROWS * LANES
GROUPS = ((1, 32), (8, 96), (24, 2), (7,))
VMEM_LIMIT = 40 * 1024 * 1024


def iota(shape, dim):
    return lax.broadcasted_iota(jnp.int32, shape, dim)


def dot(a, b, ca=1, cb=0):
    return lax.dot_general(a, b, (((ca,), (cb,)), ((), ())), preferred_element_type=F32)


def flag(mask):
    return jnp.where(mask, 1.0, 0.0).astype(BF)


def smooth(z):
    return 0.3 * z + 0.7 * (jnp.maximum(z, 0.0) + jnp.log(1.0 + jnp.exp(-jnp.abs(z))))


def slope_of(z):
    return 0.65 + 0.35 * jnp.tanh(0.5 * z)


def from_left(x):
    return jnp.where(iota(x.shape, 1) == 0, 0.0, pltpu.roll(x, 1, 1))


def from_right(x):
    return jnp.where(iota(x.shape, 1) == LANES - 1, 0.0, pltpu.roll(x, LANES - 1, 1))


def tile(h):
    return slice(h * LANES, (h + 1) * LANES)


def spot():
    at = (lax.axis_index("x") * lax.axis_size("y") + lax.axis_index("y")) * lax.axis_size("z") + lax.axis_index("z")
    return at, lax.axis_size("x") * lax.axis_size("y") * lax.axis_size("z")


def place(even_ref, odd_ref, lo_ref, hi_ref, step=1):
    at, count = spot()
    upper = lax.rem(at // step, 2) == 1

    @pl.when(upper)
    def _():
        lo_ref[...] = even_ref[...]
        hi_ref[...] = odd_ref[...]

    @pl.when(jnp.logical_not(upper))
    def _():
        lo_ref[...] = odd_ref[...]
        hi_ref[...] = even_ref[...]

    @pl.when(at < step)
    def _():
        lo_ref[...] = jnp.zeros_like(lo_ref)

    @pl.when(at >= count - step)
    def _():
        hi_ref[...] = jnp.zeros_like(hi_ref)


def pack_kernel(vol_ref, cot_ref, even_ref, odd_ref):
    cot = cot_ref[...].reshape(512, LANES)
    even_ref[0:512] = cot
    odd_ref[0:512] = cot
    at, _ = spot()
    upper = lax.rem(at, 2) == 1

    def put(even, odd):
        for ref, d in ((even_ref, even), (odd_ref, odd)):
            plane = vol_ref[:, d].reshape(128, 256)
            ref[512:640] = plane[:, 0:128]
            ref[640:768] = plane[:, 128:256]

    @pl.when(upper)
    def _():
        put(0, 1)

    @pl.when(jnp.logical_not(upper))
    def _():
        put(1, 0)


def first_kernel(
    vol_ref, even_ref, odd_ref, w_ref, b_ref, patches_ref, slope_ref, pooled_ref, lo_ref, hi_ref
):
    place(even_ref.at[512:768], odd_ref.at[512:768], lo_ref, hi_ref)
    cols = iota((256, 512), 1)
    pick_cols = flag(iota((256, 512), 0) == 2 * (cols & 127) + (cols >> 7) - 1)
    rows = iota((256, 128), 0)
    src = iota((256, 128), 1)
    pick_rows = flag(((rows & 3) == (src >> 5)) & ((src & 31) == 2 * (rows >> 4) + ((rows >> 2) & 3) - 1))
    planes = [
        jnp.concatenate([lo_ref[0:128], lo_ref[128:256]], axis=1),
        vol_ref[:, 0].reshape(128, 256),
        vol_ref[:, 1].reshape(128, 256),
        jnp.concatenate([hi_ref[0:128], hi_ref[128:256]], axis=1),
    ]
    for a in range(4):
        wide = dot(planes[a], pick_cols).astype(BF)
        both = dot(pick_rows, wide).astype(BF)
        for e in range(4):
            k = (a * 4 + e) * 16
            for h in range(ROWS):
                patches_ref[k : k + 16, tile(h)] = both[h * 16 : (h + 1) * 16, tile(e)]
    base = w_ref[...]
    weights = jnp.concatenate(
        [
            base if i == 0 else pltpu.roll(base, (i >> 2) * 64 + (i & 1) * 16 + ((i >> 1) & 1) * 4, 1)
            for i in range(8)
        ],
        axis=0,
    ).astype(BF)
    bias = b_ref[...]
    for n in range(8):
        span = slice(n * 256, (n + 1) * 256)
        pre = dot(weights, patches_ref[:, span])
        total = None
        for i in range(8):
            z = pre[i * 16 : (i + 1) * 16] + bias
            slope_ref[i * 16 : (i + 1) * 16, span] = slope_of(z)
            value = smooth(z)
            total = value if total is None else total + value
        pooled_ref[:, span] = (total * 0.125).astype(BF)


def second_kernel(
    mid_ref, near_even_ref, near_odd_ref, far_even_ref, far_odd_ref, w_ref, b_ref, cot_ref, cot_even_ref, cot_odd_ref,
    slope_ref, patches_ref, act_ref, gw_ref, p_ref, x_ref, g_ref, t_ref, s_ref, cot_lo_ref, cot_hi_ref, u_ref, up_ref, one_ref
):
    place(near_even_ref, near_odd_ref, p_ref.at[16:32], p_ref.at[48:64])
    place(far_even_ref, far_odd_ref, p_ref.at[0:16], p_ref.at[64:80], 2)
    p_ref[32:48, :] = mid_ref[...]
    place(cot_even_ref.at[0:512], cot_odd_ref.at[0:512], cot_lo_ref, cot_hi_ref)
    zero = jnp.zeros((16, LANES), BF)
    for a in range(5):
        for b in range(3):
            k = (a * 3 + b) * 16
            for h in range(ROWS):
                q = h + b - 1
                x_ref[k : k + 16, tile(h)] = p_ref[a * 16 : (a + 1) * 16, tile(q)] if 0 <= q < ROWS else zero
    w = w_ref[...].astype(F32)
    weights = jnp.concatenate(
        [
            jnp.concatenate([w[(k * 3 + e) * 16 : (k * 3 + e + 1) * 16] for e in range(3)], axis=1)
            for k in range(9)
        ],
        axis=0,
    )
    weights = jnp.transpose(weights).astype(BF)
    r = iota((512, 512), 0)
    q = iota((512, 512), 1)
    swap = flag(((r >> 5) == (q & 15)) & ((r & 31) == (q >> 4)))
    cots = jnp.concatenate([c[...].reshape(512, LANES) for c in (cot_lo_ref, cot_ref, cot_hi_ref)], axis=1)
    cots = dot(swap, cots)
    bias = b_ref[...]
    for d in range(3):
        for n in range(4):
            t_ref[...] = dot(weights, x_ref[d * 48 : d * 48 + 144, n * 512 : (n + 1) * 512])
            for j in range(4):
                h = n * 4 + j
                z = (
                    from_left(t_ref[0:32, tile(j)])
                    + t_ref[32:64, tile(j)]
                    + from_right(t_ref[64:96, tile(j)])
                    + bias
                )
                g = (cots[h * 32 : (h + 1) * 32, tile(d)] * slope_of(z)).astype(BF)
                up_ref[(2 - d) * 32 : (3 - d) * 32, tile(h)] = g
                if d == 1:
                    s_ref[h * 32 : (h + 1) * 32] = smooth(z).astype(BF)
                    g = g.astype(F32)
                    g_ref[0:32, tile(h)] = from_right(g).astype(BF)
                    g_ref[32:64, tile(h)] = g.astype(BF)
                    g_ref[64:96, tile(h)] = from_left(g).astype(BF)
    g_ref[96:128, :] = jnp.zeros((32, CELLS), BF)
    act_ref[...] = dot(swap, s_ref[...], 0, 0).astype(BF).reshape(32, ROWS, LANES)
    gw_ref[0:144] = dot(x_ref[48:192], g_ref[...], 1, 1)
    gw_ref[144:160] = dot(jnp.ones((16, CELLS), BF), g_ref[...], 1, 1)
    weights = jnp.concatenate([w[a * 144 : (a + 1) * 144] for a in range(3)], axis=1).astype(BF)
    u_ref[...] = dot(weights, up_ref[...])
    sums = jnp.zeros((16, 1), F32)
    for h in range(ROWS):
        cols = []
        for e in range(3):
            parts = [
                u_ref[(b * 3 + e) * 16 : (b * 3 + e + 1) * 16, tile(h - b + 1)]
                for b in range(3)
                if 0 <= h - b + 1 < ROWS
            ]
            cols.append(functools.reduce(lambda x, y: x + y, parts))
        gp = (from_right(cols[0]) + cols[1] + from_left(cols[2])) * 0.125
        total = None
        for i in range(8):
            g = (gp * slope_ref[i * 16 : (i + 1) * 16, tile(h)]).astype(BF)
            one_ref[i * 16 : (i + 1) * 16, tile(h)] = g
            g = g.astype(F32)
            total = g if total is None else total + g
        sums = sums + jnp.sum(total, axis=1, keepdims=True)
    full = dot(one_ref[...], patches_ref[...], 1, 1)
    acc = full[0:16]
    for i in range(1, 8):
        shift = (i >> 2) * 64 + (i & 1) * 16 + ((i >> 1) & 1) * 4
        acc = acc + pltpu.roll(full[i * 16 : (i + 1) * 16], 256 - shift, 1)
    acc = jnp.where(iota((16, 256), 1) == 255, sums, acc)
    for i in range(8):
        gw_ref[i * 16 : (i + 1) * 16, 96:128] = acc[:, i * 32 : (i + 1) * 32]


def last_kernel(mine_ref, other_ref, one_ref, bias_one_ref, two_ref, bias_two_ref):
    mine = mine_ref[...]
    other = other_ref[...]
    low = lax.axis_index("core") == 0
    v = jnp.concatenate([jnp.where(low, mine, other), jnp.where(low, other, mine)], axis=0)
    turned = jnp.transpose(jnp.concatenate([v[i * 16 : (i + 1) * 16, 96:128] for i in range(8)], axis=1))
    for a in range(3):
        for b in range(3):
            k = a * 3 + b
            for e in range(3):
                row = a * 64 + e * 16 + b * 4
                one_ref[k * 3 + e] = turned[row : row + 4]
                two_ref[k * 3 + e] = v[k * 16 : (k + 1) * 16, e * 32 : (e + 1) * 32]
    bias_one_ref[...] = turned[255:256]
    bias_two_ref[...] = v[144:145, 32:64]


def call(kernel, outs, scratch, name):
    return pl.pallas_call(
        kernel,
        out_shape=outs,
        scratch_shapes=scratch,
        compiler_params=pltpu.CompilerParams(vmem_limit_bytes=VMEM_LIMIT),
        name=name,
    )


def shape(dims, kind):
    return jax.ShapeDtypeStruct(dims, kind)


def pairs(even, odd, axis, step=1):
    n = lax.axis_size(axis)
    first = lax.ppermute(even, axis, [(i, i ^ step) for i in range(n)])
    to = [(((i + step) ^ step) - step) % n for i in range(n)]
    if step == 2:
        to[0], to[1], to[n - 2], to[n - 1] = 1, 0, n - 1, n - 2
    second = lax.ppermute(odd, axis, list(enumerate(to)))
    return first, second


def group_sum(v, axis, masks):
    n = lax.axis_size(axis)
    places = [0]
    for m in masks:
        places = places + [p ^ m for p in places]
    parts = [v if p == 0 else lax.ppermute(v, axis, [(i, i ^ p) for i in range(n)]) for p in places]
    while len(parts) > 1:
        half = len(parts) // 2
        parts = [parts[i] + parts[i + half] for i in range(half)]
    return parts[0]


def body(volumes, conv_one, bias_one, conv_two, bias_two, cotangent):
    depth = ("x", "y", "z")
    vol = volumes[0]
    cot = cotangent.reshape(32, ROWS, LANES)
    packed = shape((768, LANES), BF)
    even_part, odd_part = pairs(*call(pack_kernel, (packed, packed), [], "pack")(vol, cot), depth)
    base = jnp.pad(conv_one.astype(F32).transpose(4, 0, 2, 1, 3), ((0, 0), (0, 1), (0, 1), (0, 1), (0, 0))).reshape(16, 256)
    plane = pltpu.VMEM((256, LANES), BF)
    patches, slopes, pooled = call(
        first_kernel,
        (shape((256, CELLS), BF), shape((128, CELLS), F32), shape((16, CELLS), BF)),
        [plane, plane],
        "first",
    )(vol, even_part, odd_part, base, bias_one.reshape(16, 1))
    near = pairs(pooled, pooled, depth)
    far = pairs(pooled, pooled, depth, 2)
    act, v = call(
        second_kernel,
        (shape((32, ROWS, LANES), BF), shape((160, 128), F32)),
        [
            pltpu.VMEM((80, CELLS), BF),
            pltpu.VMEM((240, CELLS), BF),
            pltpu.VMEM((128, CELLS), BF),
            pltpu.VMEM((96, 512), F32),
            pltpu.VMEM((512, LANES), BF),
            pltpu.VMEM((512, LANES), BF),
            pltpu.VMEM((512, LANES), BF),
            pltpu.VMEM((144, CELLS), F32),
            pltpu.VMEM((96, CELLS), BF),
            pltpu.VMEM((128, CELLS), BF),
        ],
        "second",
    )(pooled, *near, *far, conv_two.reshape(432, 32), bias_two.reshape(32, 1), cot, even_part, odd_part, slopes, patches)
    low = lax.axis_index("core") == 0
    swap = [(0, 1), (1, 0)]
    v = jnp.where(low, v[:80], v[80:]) + lax.ppermute(jnp.where(low, v[80:], v[:80]), "core", swap)
    for masks in GROUPS if lax.axis_size(depth) == 128 else ((1, 2), (7,)):
        v = group_sum(v, depth, masks)
    one, sum_one, two, sum_two = call(
        last_kernel,
        (shape((27, 4, 16), F32), shape((1, 16), F32), shape((27, 16, 32), F32), shape((1, 32), F32)),
        [],
        "last",
    )(v, lax.ppermute(v, "core", swap))
    return (
        act.reshape(1, 32, 1, ROWS, LANES),
        one.reshape(3, 3, 3, 4, 16),
        sum_one.reshape(16),
        two.reshape(3, 3, 3, 16, 32),
        sum_two.reshape(32),
    )


def solution(mesh):
    devices = mesh.devices
    if devices.shape == (2, 128):
        split = (2, 4, 4, 8)
    else:
        split = (2, 1, 1, devices.shape[1])
    fine = Mesh(devices.reshape(split), ("core", "x", "y", "z"))
    cells = P("core", None, ("x", "y", "z"), None, None)
    return jax.shard_map(
        body,
        mesh=fine,
        in_specs=(cells, P(), P(), P(), P(), cells),
        out_specs=(cells, P(), P(), P(), P()),
        check_vma=False,
    )
```

```python
import functools

import jax
import jax.numpy as jnp
from jax import lax
from jax.experimental import pallas as pl
from jax.experimental.pallas import tpu as pltpu
from jax.sharding import Mesh, PartitionSpec as P

BF = jnp.bfloat16
F32 = jnp.float32
ROWS = 16
LANES = 128
CELLS = ROWS * LANES
GROUPS = ((1, 32), (8, 96), (24, 2), (7,))
VMEM_LIMIT = 40 * 1024 * 1024


def iota(shape, dim):
    return lax.broadcasted_iota(jnp.int32, shape, dim)


def dot(a, b, ca=1, cb=0):
    return lax.dot_general(a, b, (((ca,), (cb,)), ((), ())), preferred_element_type=F32)


def flag(mask):
    return jnp.where(mask, 1.0, 0.0).astype(BF)


def smooth(z):
    return 0.3 * z + 0.7 * (jnp.maximum(z, 0.0) + jnp.log(1.0 + jnp.exp(-jnp.abs(z))))


def slope_of(z):
    return 0.65 + 0.35 * jnp.tanh(0.5 * z)


def from_left(x):
    return jnp.where(iota(x.shape, 1) == 0, 0.0, pltpu.roll(x, 1, 1))


def from_right(x):
    return jnp.where(iota(x.shape, 1) == LANES - 1, 0.0, pltpu.roll(x, LANES - 1, 1))


def tile(h):
    return slice(h * LANES, (h + 1) * LANES)


def spot():
    at = (lax.axis_index("x") * lax.axis_size("y") + lax.axis_index("y")) * lax.axis_size("z") + lax.axis_index("z")
    return at, lax.axis_size("x") * lax.axis_size("y") * lax.axis_size("z")


def place(even_ref, odd_ref, lo_ref, hi_ref, step=1):
    at, count = spot()
    upper = lax.rem(at // step, 2) == 1

    @pl.when(upper)
    def _():
        lo_ref[...] = even_ref[...]
        hi_ref[...] = odd_ref[...]

    @pl.when(jnp.logical_not(upper))
    def _():
        lo_ref[...] = odd_ref[...]
        hi_ref[...] = even_ref[...]

    @pl.when(at < step)
    def _():
        lo_ref[...] = jnp.zeros_like(lo_ref)

    @pl.when(at >= count - step)
    def _():
        hi_ref[...] = jnp.zeros_like(hi_ref)


def pack_kernel(vol_ref, cot_ref, even_ref, odd_ref):
    cot = cot_ref[...].reshape(512, LANES)
    even_ref[0:512] = cot
    odd_ref[0:512] = cot
    at, _ = spot()
    upper = lax.rem(at, 2) == 1

    def put(even, odd):
        for ref, d in ((even_ref, even), (odd_ref, odd)):
            plane = vol_ref[:, d].reshape(128, 256)
            ref[512:640] = plane[:, 0:128]
            ref[640:768] = plane[:, 128:256]

    @pl.when(upper)
    def _():
        put(0, 1)

    @pl.when(jnp.logical_not(upper))
    def _():
        put(1, 0)


def first_kernel(
    vol_ref, even_ref, odd_ref, w_ref, b_ref, patches_ref, slope_ref, pooled_ref, lo_ref, hi_ref
):
    place(even_ref.at[512:768], odd_ref.at[512:768], lo_ref, hi_ref)
    cols = iota((256, 512), 1)
    pick_cols = flag(iota((256, 512), 0) == 2 * (cols & 127) + (cols >> 7) - 1)
    rows = iota((256, 128), 0)
    src = iota((256, 128), 1)
    pick_rows = flag(((rows & 3) == (src >> 5)) & ((src & 31) == 2 * (rows >> 4) + ((rows >> 2) & 3) - 1))
    planes = [
        jnp.concatenate([lo_ref[0:128], lo_ref[128:256]], axis=1),
        vol_ref[:, 0].reshape(128, 256),
        vol_ref[:, 1].reshape(128, 256),
        jnp.concatenate([hi_ref[0:128], hi_ref[128:256]], axis=1),
    ]
    for a in range(4):
        wide = dot(planes[a], pick_cols).astype(BF)
        both = dot(pick_rows, wide).astype(BF)
        for e in range(4):
            k = (a * 4 + e) * 16
            for h in range(ROWS):
                patches_ref[k : k + 16, tile(h)] = both[h * 16 : (h + 1) * 16, tile(e)]
    base = w_ref[...]
    weights = jnp.concatenate(
        [
            base if i == 0 else pltpu.roll(base, (i >> 2) * 64 + (i & 1) * 16 + ((i >> 1) & 1) * 4, 1)
            for i in range(8)
        ],
        axis=0,
    ).astype(BF)
    bias = b_ref[...]
    for n in range(8):
        span = slice(n * 256, (n + 1) * 256)
        pre = dot(weights, patches_ref[:, span])
        total = None
        for i in range(8):
            z = pre[i * 16 : (i + 1) * 16] + bias
            slope_ref[i * 16 : (i + 1) * 16, span] = slope_of(z)
            value = smooth(z)
            total = value if total is None else total + value
        pooled_ref[:, span] = (total * 0.125).astype(BF)


def second_kernel(
    mid_ref, near_even_ref, far_even_ref, near_odd_ref, far_odd_ref, w_ref, b_ref, cot_ref, cot_even_ref, cot_odd_ref,
    slope_ref, patches_ref, act_ref, gw_ref, p_ref, x_ref, g_ref, t_ref, s_ref, cot_lo_ref, cot_hi_ref, u_ref, up_ref, one_ref
):
    place(near_even_ref, near_odd_ref, p_ref.at[16:32], p_ref.at[48:64])
    place(far_even_ref, far_odd_ref, p_ref.at[0:16], p_ref.at[64:80], 2)
    p_ref[32:48, :] = mid_ref[...]
    place(cot_even_ref.at[0:512], cot_odd_ref.at[0:512], cot_lo_ref, cot_hi_ref)
    zero = jnp.zeros((16, LANES), BF)
    for a in range(5):
        for b in range(3):
            k = (a * 3 + b) * 16
            for h in range(ROWS):
                q = h + b - 1
                x_ref[k : k + 16, tile(h)] = p_ref[a * 16 : (a + 1) * 16, tile(q)] if 0 <= q < ROWS else zero
    w = w_ref[...].astype(F32)
    weights = jnp.concatenate(
        [
            jnp.concatenate([w[(k * 3 + e) * 16 : (k * 3 + e + 1) * 16] for e in range(3)], axis=1)
            for k in range(9)
        ],
        axis=0,
    )
    weights = jnp.transpose(weights).astype(BF)
    r = iota((512, 512), 0)
    q = iota((512, 512), 1)
    swap = flag(((r >> 5) == (q & 15)) & ((r & 31) == (q >> 4)))
    cots = jnp.concatenate([c[...].reshape(512, LANES) for c in (cot_lo_ref, cot_ref, cot_hi_ref)], axis=1)
    cots = dot(swap, cots)
    bias = b_ref[...]
    for d in range(3):
        for n in range(4):
            t_ref[...] = dot(weights, x_ref[d * 48 : d * 48 + 144, n * 512 : (n + 1) * 512])
            for j in range(4):
                h = n * 4 + j
                z = (
                    from_left(t_ref[0:32, tile(j)])
                    + t_ref[32:64, tile(j)]
                    + from_right(t_ref[64:96, tile(j)])
                    + bias
                )
                g = (cots[h * 32 : (h + 1) * 32, tile(d)] * slope_of(z)).astype(BF)
                up_ref[(2 - d) * 32 : (3 - d) * 32, tile(h)] = g
                if d == 1:
                    s_ref[h * 32 : (h + 1) * 32] = smooth(z).astype(BF)
                    g = g.astype(F32)
                    g_ref[0:32, tile(h)] = from_right(g).astype(BF)
                    g_ref[32:64, tile(h)] = g.astype(BF)
                    g_ref[64:96, tile(h)] = from_left(g).astype(BF)
    g_ref[96:128, :] = jnp.zeros((32, CELLS), BF)
    act_ref[...] = dot(swap, s_ref[...], 0, 0).astype(BF).reshape(32, ROWS, LANES)
    gw_ref[0:144] = dot(x_ref[48:192], g_ref[...], 1, 1)
    gw_ref[144:160] = dot(jnp.ones((16, CELLS), BF), g_ref[...], 1, 1)
    weights = jnp.concatenate([w[a * 144 : (a + 1) * 144] for a in range(3)], axis=1).astype(BF)
    u_ref[...] = dot(weights, up_ref[...])
    sums = jnp.zeros((16, 1), F32)
    for h in range(ROWS):
        cols = []
        for e in range(3):
            parts = [
                u_ref[(b * 3 + e) * 16 : (b * 3 + e + 1) * 16, tile(h - b + 1)]
                for b in range(3)
                if 0 <= h - b + 1 < ROWS
            ]
            cols.append(functools.reduce(lambda x, y: x + y, parts))
        gp = (from_right(cols[0]) + cols[1] + from_left(cols[2])) * 0.125
        total = None
        for i in range(8):
            g = (gp * slope_ref[i * 16 : (i + 1) * 16, tile(h)]).astype(BF)
            one_ref[i * 16 : (i + 1) * 16, tile(h)] = g
            g = g.astype(F32)
            total = g if total is None else total + g
        sums = sums + jnp.sum(total, axis=1, keepdims=True)
    full = dot(one_ref[...], patches_ref[...], 1, 1)
    acc = full[0:16]
    for i in range(1, 8):
        shift = (i >> 2) * 64 + (i & 1) * 16 + ((i >> 1) & 1) * 4
        acc = acc + pltpu.roll(full[i * 16 : (i + 1) * 16], 256 - shift, 1)
    acc = jnp.where(iota((16, 256), 1) == 255, sums, acc)
    for i in range(8):
        gw_ref[i * 16 : (i + 1) * 16, 96:128] = acc[:, i * 32 : (i + 1) * 32]


def last_kernel(mine_ref, other_ref, one_ref, bias_one_ref, two_ref, bias_two_ref):
    mine = mine_ref[...]
    other = other_ref[...]
    low = lax.axis_index("core") == 0
    v = jnp.concatenate([jnp.where(low, mine, other), jnp.where(low, other, mine)], axis=0)
    turned = jnp.transpose(jnp.concatenate([v[i * 16 : (i + 1) * 16, 96:128] for i in range(8)], axis=1))
    for a in range(3):
        for b in range(3):
            k = a * 3 + b
            for e in range(3):
                row = a * 64 + e * 16 + b * 4
                one_ref[k * 3 + e] = turned[row : row + 4]
                two_ref[k * 3 + e] = v[k * 16 : (k + 1) * 16, e * 32 : (e + 1) * 32]
    bias_one_ref[...] = turned[255:256]
    bias_two_ref[...] = v[144:145, 32:64]


def call(kernel, outs, scratch, name):
    return pl.pallas_call(
        kernel,
        out_shape=outs,
        scratch_shapes=scratch,
        compiler_params=pltpu.CompilerParams(vmem_limit_bytes=VMEM_LIMIT),
        name=name,
    )


def shape(dims, kind):
    return jax.ShapeDtypeStruct(dims, kind)


def even_swap(v, axis, step=1):
    return lax.ppermute(v, axis, [(i, i ^ step) for i in range(lax.axis_size(axis))])


def odd_swap(v, axis, step=1):
    n = lax.axis_size(axis)
    to = [(((i + step) ^ step) - step) % n for i in range(n)]
    if step == 2:
        to[0], to[1], to[n - 2], to[n - 1] = 1, 0, n - 1, n - 2
    return lax.ppermute(v, axis, list(enumerate(to)))


def group_sum(v, axis, masks):
    n = lax.axis_size(axis)
    places = [0]
    for m in masks:
        places = places + [p ^ m for p in places]
    parts = [v if p == 0 else lax.ppermute(v, axis, [(i, i ^ p) for i in range(n)]) for p in places]
    while len(parts) > 1:
        half = len(parts) // 2
        parts = [parts[i] + parts[i + half] for i in range(half)]
    return parts[0]


def body(volumes, conv_one, bias_one, conv_two, bias_two, cotangent):
    depth = ("x", "y", "z")
    vol = volumes[0]
    cot = cotangent.reshape(32, ROWS, LANES)
    packed = shape((768, LANES), BF)
    even_part, odd_part = call(pack_kernel, (packed, packed), [], "pack")(vol, cot)
    even_part, odd_part = even_swap(even_part, depth), odd_swap(odd_part, depth)
    base = jnp.pad(conv_one.astype(F32).transpose(4, 0, 2, 1, 3), ((0, 0), (0, 1), (0, 1), (0, 1), (0, 0))).reshape(16, 256)
    plane = pltpu.VMEM((256, LANES), BF)
    patches, slopes, pooled = call(
        first_kernel,
        (shape((256, CELLS), BF), shape((128, CELLS), F32), shape((16, CELLS), BF)),
        [plane, plane],
        "first",
    )(vol, even_part, odd_part, base, bias_one.reshape(16, 1))
    near_even, far_even = even_swap(pooled, depth), even_swap(pooled, depth, 2)
    near_odd, far_odd = odd_swap(pooled, depth), odd_swap(pooled, depth, 2)
    act, v = call(
        second_kernel,
        (shape((32, ROWS, LANES), BF), shape((160, 128), F32)),
        [
            pltpu.VMEM((80, CELLS), BF),
            pltpu.VMEM((240, CELLS), BF),
            pltpu.VMEM((128, CELLS), BF),
            pltpu.VMEM((96, 512), F32),
            pltpu.VMEM((512, LANES), BF),
            pltpu.VMEM((512, LANES), BF),
            pltpu.VMEM((512, LANES), BF),
            pltpu.VMEM((144, CELLS), F32),
            pltpu.VMEM((96, CELLS), BF),
            pltpu.VMEM((128, CELLS), BF),
        ],
        "second",
    )(pooled, near_even, far_even, near_odd, far_odd, conv_two.reshape(432, 32), bias_two.reshape(32, 1), cot, even_part, odd_part, slopes, patches)
    low = lax.axis_index("core") == 0
    swap = [(0, 1), (1, 0)]
    v = jnp.where(low, v[:80], v[80:]) + lax.ppermute(jnp.where(low, v[80:], v[:80]), "core", swap)
    for masks in GROUPS if lax.axis_size(depth) == 128 else ((1, 2), (7,)):
        v = group_sum(v, depth, masks)
    one, sum_one, two, sum_two = call(
        last_kernel,
        (shape((27, 4, 16), F32), shape((1, 16), F32), shape((27, 16, 32), F32), shape((1, 32), F32)),
        [],
        "last",
    )(v, lax.ppermute(v, "core", swap))
    return (
        act.reshape(1, 32, 1, ROWS, LANES),
        one.reshape(3, 3, 3, 4, 16),
        sum_one.reshape(16),
        two.reshape(3, 3, 3, 16, 32),
        sum_two.reshape(32),
    )


def solution(mesh):
    devices = mesh.devices
    if devices.shape == (2, 128):
        split = (2, 4, 4, 8)
    else:
        split = (2, 1, 1, devices.shape[1])
    fine = Mesh(devices.reshape(split), ("core", "x", "y", "z"))
    cells = P("core", None, ("x", "y", "z"), None, None)
    return jax.shard_map(
        body,
        mesh=fine,
        in_specs=(cells, P(), P(), P(), P(), cells),
        out_specs=(cells, P(), P(), P(), P()),
        check_vma=False,
    )
```

```python
import functools

import jax
import jax.numpy as jnp
from jax import lax
from jax.experimental import pallas as pl
from jax.experimental.pallas import tpu as pltpu
from jax.sharding import Mesh, PartitionSpec as P

BF = jnp.bfloat16
F32 = jnp.float32
ROWS = 16
LANES = 128
CELLS = ROWS * LANES
GROUPS = ((1, 32), (8, 96), (24, 2), (7,))
VMEM_LIMIT = 40 * 1024 * 1024


def iota(shape, dim):
    return lax.broadcasted_iota(jnp.int32, shape, dim)


def dot(a, b, ca=1, cb=0):
    return lax.dot_general(a, b, (((ca,), (cb,)), ((), ())), preferred_element_type=F32)


def flag(mask):
    return jnp.where(mask, 1.0, 0.0).astype(BF)


def smooth(z):
    return 0.3 * z + 0.7 * (jnp.maximum(z, 0.0) + jnp.log(1.0 + jnp.exp(-jnp.abs(z))))


def slope_of(z):
    return 0.65 + 0.35 * jnp.tanh(0.5 * z)


def from_left(x):
    return jnp.where(iota(x.shape, 1) == 0, 0.0, pltpu.roll(x, 1, 1))


def from_right(x):
    return jnp.where(iota(x.shape, 1) == LANES - 1, 0.0, pltpu.roll(x, LANES - 1, 1))


def tile(h):
    return slice(h * LANES, (h + 1) * LANES)


def spot():
    at = (lax.axis_index("x") * lax.axis_size("y") + lax.axis_index("y")) * lax.axis_size("z") + lax.axis_index("z")
    return at, lax.axis_size("x") * lax.axis_size("y") * lax.axis_size("z")


def place(even_ref, odd_ref, lo_ref, hi_ref, step=1):
    at, count = spot()
    upper = lax.rem(at // step, 2) == 1

    @pl.when(upper)
    def _():
        lo_ref[...] = even_ref[...]
        hi_ref[...] = odd_ref[...]

    @pl.when(jnp.logical_not(upper))
    def _():
        lo_ref[...] = odd_ref[...]
        hi_ref[...] = even_ref[...]

    @pl.when(at < step)
    def _():
        lo_ref[...] = jnp.zeros_like(lo_ref)

    @pl.when(at >= count - step)
    def _():
        hi_ref[...] = jnp.zeros_like(hi_ref)


def pack_kernel(vol_ref, cot_ref, even_ref, odd_ref):
    cot = cot_ref[...].reshape(512, LANES)
    even_ref[0:512] = cot
    odd_ref[0:512] = cot
    at, _ = spot()
    upper = lax.rem(at, 2) == 1

    def put(even, odd):
        for ref, d in ((even_ref, even), (odd_ref, odd)):
            plane = vol_ref[:, d].reshape(128, 256)
            ref[512:640] = plane[:, 0:128]
            ref[640:768] = plane[:, 128:256]

    @pl.when(upper)
    def _():
        put(0, 1)

    @pl.when(jnp.logical_not(upper))
    def _():
        put(1, 0)


def first_kernel(
    vol_ref, odd_ref, even_ref, w_ref, b_ref, patches_ref, slope_ref, pooled_ref, lo_ref, hi_ref
):
    place(even_ref.at[512:768], odd_ref.at[512:768], lo_ref, hi_ref)
    cols = iota((256, 512), 1)
    pick_cols = flag(iota((256, 512), 0) == 2 * (cols & 127) + (cols >> 7) - 1)
    rows = iota((256, 128), 0)
    src = iota((256, 128), 1)
    pick_rows = flag(((rows & 3) == (src >> 5)) & ((src & 31) == 2 * (rows >> 4) + ((rows >> 2) & 3) - 1))
    planes = [
        jnp.concatenate([lo_ref[0:128], lo_ref[128:256]], axis=1),
        vol_ref[:, 0].reshape(128, 256),
        vol_ref[:, 1].reshape(128, 256),
        jnp.concatenate([hi_ref[0:128], hi_ref[128:256]], axis=1),
    ]
    for a in range(4):
        wide = dot(planes[a], pick_cols).astype(BF)
        both = dot(pick_rows, wide).astype(BF)
        for e in range(4):
            k = (a * 4 + e) * 16
            for h in range(ROWS):
                patches_ref[k : k + 16, tile(h)] = both[h * 16 : (h + 1) * 16, tile(e)]
    base = w_ref[...]
    weights = jnp.concatenate(
        [
            base if i == 0 else pltpu.roll(base, (i >> 2) * 64 + (i & 1) * 16 + ((i >> 1) & 1) * 4, 1)
            for i in range(8)
        ],
        axis=0,
    ).astype(BF)
    bias = b_ref[...]
    for n in range(8):
        span = slice(n * 256, (n + 1) * 256)
        pre = dot(weights, patches_ref[:, span])
        total = None
        for i in range(8):
            z = pre[i * 16 : (i + 1) * 16] + bias
            slope_ref[i * 16 : (i + 1) * 16, span] = slope_of(z)
            value = smooth(z)
            total = value if total is None else total + value
        pooled_ref[:, span] = (total * 0.125).astype(BF)


def second_kernel(
    mid_ref, near_odd_ref, far_odd_ref, near_even_ref, far_even_ref, w_ref, b_ref, cot_ref, cot_even_ref, cot_odd_ref,
    slope_ref, patches_ref, act_ref, gw_ref, p_ref, x_ref, g_ref, t_ref, s_ref, cot_lo_ref, cot_hi_ref, u_ref, up_ref, one_ref
):
    place(near_even_ref, near_odd_ref, p_ref.at[16:32], p_ref.at[48:64])
    place(far_even_ref, far_odd_ref, p_ref.at[0:16], p_ref.at[64:80], 2)
    p_ref[32:48, :] = mid_ref[...]
    place(cot_even_ref.at[0:512], cot_odd_ref.at[0:512], cot_lo_ref, cot_hi_ref)
    zero = jnp.zeros((16, LANES), BF)
    for a in range(5):
        for b in range(3):
            k = (a * 3 + b) * 16
            for h in range(ROWS):
                q = h + b - 1
                x_ref[k : k + 16, tile(h)] = p_ref[a * 16 : (a + 1) * 16, tile(q)] if 0 <= q < ROWS else zero
    w = w_ref[...].astype(F32)
    weights = jnp.concatenate(
        [
            jnp.concatenate([w[(k * 3 + e) * 16 : (k * 3 + e + 1) * 16] for e in range(3)], axis=1)
            for k in range(9)
        ],
        axis=0,
    )
    weights = jnp.transpose(weights).astype(BF)
    r = iota((512, 512), 0)
    q = iota((512, 512), 1)
    swap = flag(((r >> 5) == (q & 15)) & ((r & 31) == (q >> 4)))
    cots = jnp.concatenate([c[...].reshape(512, LANES) for c in (cot_lo_ref, cot_ref, cot_hi_ref)], axis=1)
    cots = dot(swap, cots)
    bias = b_ref[...]
    for d in range(3):
        for n in range(4):
            t_ref[...] = dot(weights, x_ref[d * 48 : d * 48 + 144, n * 512 : (n + 1) * 512])
            for j in range(4):
                h = n * 4 + j
                z = (
                    from_left(t_ref[0:32, tile(j)])
                    + t_ref[32:64, tile(j)]
                    + from_right(t_ref[64:96, tile(j)])
                    + bias
                )
                g = (cots[h * 32 : (h + 1) * 32, tile(d)] * slope_of(z)).astype(BF)
                up_ref[(2 - d) * 32 : (3 - d) * 32, tile(h)] = g
                if d == 1:
                    s_ref[h * 32 : (h + 1) * 32] = smooth(z).astype(BF)
                    g = g.astype(F32)
                    g_ref[0:32, tile(h)] = from_right(g).astype(BF)
                    g_ref[32:64, tile(h)] = g.astype(BF)
                    g_ref[64:96, tile(h)] = from_left(g).astype(BF)
    g_ref[96:128, :] = jnp.zeros((32, CELLS), BF)
    act_ref[...] = dot(swap, s_ref[...], 0, 0).astype(BF).reshape(32, ROWS, LANES)
    gw_ref[0:144] = dot(x_ref[48:192], g_ref[...], 1, 1)
    gw_ref[144:160] = dot(jnp.ones((16, CELLS), BF), g_ref[...], 1, 1)
    weights = jnp.concatenate([w[a * 144 : (a + 1) * 144] for a in range(3)], axis=1).astype(BF)
    u_ref[...] = dot(weights, up_ref[...])
    sums = jnp.zeros((16, 1), F32)
    for h in range(ROWS):
        cols = []
        for e in range(3):
            parts = [
                u_ref[(b * 3 + e) * 16 : (b * 3 + e + 1) * 16, tile(h - b + 1)]
                for b in range(3)
                if 0 <= h - b + 1 < ROWS
            ]
            cols.append(functools.reduce(lambda x, y: x + y, parts))
        gp = (from_right(cols[0]) + cols[1] + from_left(cols[2])) * 0.125
        total = None
        for i in range(8):
            g = (gp * slope_ref[i * 16 : (i + 1) * 16, tile(h)]).astype(BF)
            one_ref[i * 16 : (i + 1) * 16, tile(h)] = g
            g = g.astype(F32)
            total = g if total is None else total + g
        sums = sums + jnp.sum(total, axis=1, keepdims=True)
    full = dot(one_ref[...], patches_ref[...], 1, 1)
    acc = full[0:16]
    for i in range(1, 8):
        shift = (i >> 2) * 64 + (i & 1) * 16 + ((i >> 1) & 1) * 4
        acc = acc + pltpu.roll(full[i * 16 : (i + 1) * 16], 256 - shift, 1)
    acc = jnp.where(iota((16, 256), 1) == 255, sums, acc)
    for i in range(8):
        gw_ref[i * 16 : (i + 1) * 16, 96:128] = acc[:, i * 32 : (i + 1) * 32]


def last_kernel(mine_ref, other_ref, one_ref, bias_one_ref, two_ref, bias_two_ref):
    mine = mine_ref[...]
    other = other_ref[...]
    low = lax.axis_index("core") == 0
    v = jnp.concatenate([jnp.where(low, mine, other), jnp.where(low, other, mine)], axis=0)
    turned = jnp.transpose(jnp.concatenate([v[i * 16 : (i + 1) * 16, 96:128] for i in range(8)], axis=1))
    for a in range(3):
        for b in range(3):
            k = a * 3 + b
            for e in range(3):
                row = a * 64 + e * 16 + b * 4
                one_ref[k * 3 + e] = turned[row : row + 4]
                two_ref[k * 3 + e] = v[k * 16 : (k + 1) * 16, e * 32 : (e + 1) * 32]
    bias_one_ref[...] = turned[255:256]
    bias_two_ref[...] = v[144:145, 32:64]


def call(kernel, outs, scratch, name):
    return pl.pallas_call(
        kernel,
        out_shape=outs,
        scratch_shapes=scratch,
        compiler_params=pltpu.CompilerParams(vmem_limit_bytes=VMEM_LIMIT),
        name=name,
    )


def shape(dims, kind):
    return jax.ShapeDtypeStruct(dims, kind)


def even_swap(v, axis, step=1):
    return lax.ppermute(v, axis, [(i, i ^ step) for i in range(lax.axis_size(axis))])


def odd_swap(v, axis, step=1):
    n = lax.axis_size(axis)
    to = [(((i + step) ^ step) - step) % n for i in range(n)]
    if step == 2:
        to[0], to[1], to[n - 2], to[n - 1] = 1, 0, n - 1, n - 2
    return lax.ppermute(v, axis, list(enumerate(to)))


def group_sum(v, axis, masks):
    n = lax.axis_size(axis)
    places = [0]
    for m in masks:
        places = places + [p ^ m for p in places]
    parts = [v if p == 0 else lax.ppermute(v, axis, [(i, i ^ p) for i in range(n)]) for p in places]
    while len(parts) > 1:
        half = len(parts) // 2
        parts = [parts[i] + parts[i + half] for i in range(half)]
    return parts[0]


def body(volumes, conv_one, bias_one, conv_two, bias_two, cotangent):
    depth = ("x", "y", "z")
    vol = volumes[0]
    cot = cotangent.reshape(32, ROWS, LANES)
    packed = shape((768, LANES), BF)
    even_part, odd_part = call(pack_kernel, (packed, packed), [], "pack")(vol, cot)
    odd_part, even_part = odd_swap(odd_part, depth), even_swap(even_part, depth)
    base = jnp.pad(conv_one.astype(F32).transpose(4, 0, 2, 1, 3), ((0, 0), (0, 1), (0, 1), (0, 1), (0, 0))).reshape(16, 256)
    plane = pltpu.VMEM((256, LANES), BF)
    patches, slopes, pooled = call(
        first_kernel,
        (shape((256, CELLS), BF), shape((128, CELLS), F32), shape((16, CELLS), BF)),
        [plane, plane],
        "first",
    )(vol, odd_part, even_part, base, bias_one.reshape(16, 1))
    near_odd, far_odd = odd_swap(pooled, depth), odd_swap(pooled, depth, 2)
    near_even, far_even = even_swap(pooled, depth), even_swap(pooled, depth, 2)
    act, v = call(
        second_kernel,
        (shape((32, ROWS, LANES), BF), shape((160, 128), F32)),
        [
            pltpu.VMEM((80, CELLS), BF),
            pltpu.VMEM((240, CELLS), BF),
            pltpu.VMEM((128, CELLS), BF),
            pltpu.VMEM((96, 512), F32),
            pltpu.VMEM((512, LANES), BF),
            pltpu.VMEM((512, LANES), BF),
            pltpu.VMEM((512, LANES), BF),
            pltpu.VMEM((144, CELLS), F32),
            pltpu.VMEM((96, CELLS), BF),
            pltpu.VMEM((128, CELLS), BF),
        ],
        "second",
    )(pooled, near_odd, far_odd, near_even, far_even, conv_two.reshape(432, 32), bias_two.reshape(32, 1), cot, even_part, odd_part, slopes, patches)
    low = lax.axis_index("core") == 0
    swap = [(0, 1), (1, 0)]
    v = jnp.where(low, v[:80], v[80:]) + lax.ppermute(jnp.where(low, v[80:], v[:80]), "core", swap)
    for masks in GROUPS if lax.axis_size(depth) == 128 else ((1, 2), (7,)):
        v = group_sum(v, depth, masks)
    one, sum_one, two, sum_two = call(
        last_kernel,
        (shape((27, 4, 16), F32), shape((1, 16), F32), shape((27, 16, 32), F32), shape((1, 32), F32)),
        [],
        "last",
    )(v, lax.ppermute(v, "core", swap))
    return (
        act.reshape(1, 32, 1, ROWS, LANES),
        one.reshape(3, 3, 3, 4, 16),
        sum_one.reshape(16),
        two.reshape(3, 3, 3, 16, 32),
        sum_two.reshape(32),
    )


def solution(mesh):
    devices = mesh.devices
    if devices.shape == (2, 128):
        split = (2, 4, 4, 8)
    else:
        split = (2, 1, 1, devices.shape[1])
    fine = Mesh(devices.reshape(split), ("core", "x", "y", "z"))
    cells = P("core", None, ("x", "y", "z"), None, None)
    return jax.shard_map(
        body,
        mesh=fine,
        in_specs=(cells, P(), P(), P(), P(), cells),
        out_specs=(cells, P(), P(), P(), P()),
        check_vma=False,
    )
```
